128 devices in a mesh: lon: 32 (over x, y_hi, z), lat: 4 (over y_lo, core).
Axes of the slice: x: 4, y: 4 (y_hi: 2, y_lo: 2; y = y_hi * 2 + y_lo), z: 4, core: 2. Of those that a mesh axis runs over, the one named last changes fastest.
Arguments:
- states: bfloat16 [2, 64, 2048, 192], P(None, 'lat', 'lon'), may hold values from -6 to 6
- grad_out: bfloat16 [64, 2048, 192], P('lat', 'lon'), may hold values from -6 to 6
- land_mask: int32 [64, 2048], P('lat', 'lon'), may hold values 0 or 1
- partner: int32 [2048], replicated, may hold values from 0 to 2047, as said below
- dw_kernel: float32 [7, 7, 192], replicated, may hold values from -0.875 to 0.875
- dw_bias: float32 [192], replicated, may hold values from -3 to 3
- ln_gain: float32 [192], replicated, may hold values from 0.1 to 1.9
- ln_bias: float32 [192], replicated, may hold values from -2 to 2
- w_in: bfloat16 [192, 768], replicated, may hold values from -0.4375 to 0.4375
- b_in: float32 [768], replicated, may hold values from -2 to 2
- w_out: bfloat16 [768, 192], replicated, may hold values from -0.21875 to 0.21875
- b_out: float32 [192], replicated, may hold values from -2 to 2
- layer_scale: float32 [192], replicated, may hold values from 0.3 to 1
Outputs:
- out_a: bfloat16 [64, 2048, 192], P('lat', 'lon')
- grad_states: float32 [64, 2048, 192], P('lat', 'lon')
- grad_kernel: float32 [7, 7, 192], replicated
- grad_win: float32 [192, 768], replicated
- grad_wout: float32 [768, 192], replicated
The draws below stay inside these ranges and needn't reach their ends.
Inputs may be any that keep to these rules, and one draw needn't show every extreme that they name: partner[j] = (2047 - j + s) mod 2048 for one shift s, the same for all j: a mirror of the columns, so each column appears exactly once.
All inputs are finite; a program needn't handle non-finite values. No bound on the sum of `land_mask` on one device may be relied on, other than what follows from the above.
Results may differ from the reference program's by a relative error of at most 0.0062.
Values may be sent and summed in bfloat16 or wider, within the bound.
A program may use at most 192 MiB of HBM per device.

```python
import math
import jax
import jax.numpy as jnp
from jax import lax

CH = 192
HID = 768
NLAT = 64
NLON = 2048


def draw_partner(key, part):
    key = jax.random.fold_in(key, 11)
    shift = jax.random.randint(key, (), 0, NLON, dtype=jnp.int32)
    columns = jnp.arange(NLON, dtype=jnp.int32)
    return ((NLON - 1 - columns + shift) % NLON).astype(jnp.int32)


def touch_ends(entries, rng, low, high):
    spot = [jax.random.randint(jax.random.fold_in(rng, axis), (), 0, length) for axis, length in enumerate(entries.shape)]
    widest = entries.shape.index(max(entries.shape))
    neighbour = spot[:widest] + [(spot[widest] + 1) % entries.shape[widest]] + spot[widest + 1:]
    return entries.at[tuple(spot)].set(low).at[tuple(neighbour)].set(high)


def shard_levels(rng, extent, shards, least, largest):
    def one(position, parts):
        steps = jax.random.uniform(jax.random.fold_in(jax.random.fold_in(rng, 6), position), (parts,), jnp.float32, least / len(shards), largest / len(shards))
        return jnp.repeat(jnp.exp(steps), extent[position] // parts).reshape((-1,) + (1,) * (len(extent) - position - 1))

    factor_of = one(*shards[0])
    for cut in shards[1:]:
        factor_of = factor_of * one(*cut)
    return factor_of


def gaussian(stream_key, extent, deviation, bound, split=(), kind=jnp.bfloat16):
    entries = jax.random.normal(stream_key, extent, jnp.float32) * deviation
    if len(split) > 0:
        entries = shard_levels(stream_key, extent, split, -0.22, 0.18) * entries
    return jnp.clip(entries, min=-bound, max=bound).astype(kind)


def setup_inputs(seed: int = 0) -> dict:
    seeds = jax.random.split(jax.random.key(seed), 14)
    states = gaussian(seeds[0], (2, NLAT, NLON, CH), 1.0, 6.0, ((1, 4), (2, 32)))
    grad_out = gaussian(seeds[1], (NLAT, NLON, CH), 1.0, 6.0, ((0, 4), (1, 32)))
    land_mask = touch_ends((jax.random.randint(seeds[2], (NLAT, NLON), 0, 3) < 2).astype(jnp.int32), jax.random.fold_in(seeds[2], 1), 0, 1)
    partner = draw_partner(jax.random.fold_in(seeds[13], 71), 0)
    dw_kernel = gaussian(seeds[4], (7, 7, CH), 49 ** -0.5, 0.875, (), jnp.float32)
    dw_bias = gaussian(seeds[5], (CH,), 0.5, 3.0, (), jnp.float32)
    ln_gain = jnp.clip(1.0 + 0.18 * jax.random.normal(seeds[6], (CH,), jnp.float32), 0.1, 1.9)
    ln_bias = gaussian(seeds[7], (CH,), 0.3, 2.0, (), jnp.float32)
    w_in = gaussian(seeds[8], (CH, HID), CH ** -0.5, 0.4375)
    b_in = gaussian(seeds[9], (HID,), 0.3, 2.0, (), jnp.float32)
    w_out = gaussian(seeds[10], (HID, CH), HID ** -0.5, 0.21875)
    b_out = gaussian(seeds[11], (CH,), 0.3, 2.0, (), jnp.float32)
    layer_scale = jnp.clip(jnp.exp(jax.random.uniform(seeds[12], (CH,), jnp.float32, math.log(0.3), math.log(1.0))), 0.3, 1.0)
    return dict(states=states, grad_out=grad_out, land_mask=land_mask, partner=partner, dw_kernel=dw_kernel, dw_bias=dw_bias, ln_gain=ln_gain, ln_bias=ln_bias, w_in=w_in, b_in=b_in, w_out=w_out, b_out=b_out, layer_scale=layer_scale)


root_factor = math.sqrt(2.0 / math.pi)
cubic_coef = 0.044715
norm_eps = 1e-06

def gelu_pair(hidden):
    tangent = jnp.tanh(root_factor * (hidden + cubic_coef * hidden * hidden * hidden))
    value = 0.5 * hidden * (1.0 + tangent)
    slope = 0.5 * (1.0 + tangent) + 0.5 * hidden * (1.0 - tangent * tangent) * root_factor * (1.0 + 3.0 * cubic_coef * hidden * hidden)
    return (value, slope)

def cell_forward(depth_out, ln_gain, ln_bias, w_in, b_in, w_out, b_out):
    centre = lax.optimization_barrier(jnp.mean(depth_out, axis=-1, keepdims=True))
    centred = depth_out - centre
    inv_std = lax.rsqrt(lax.optimization_barrier(jnp.mean(centred * centred, axis=-1, keepdims=True)) + norm_eps)
    normed = centred * inv_std
    lowered = (normed * ln_gain + ln_bias).astype(jnp.bfloat16)
    hidden = jnp.dot(lowered, w_in, preferred_element_type=jnp.float32) + b_in
    value, slope = gelu_pair(hidden)
    active = value.astype(jnp.bfloat16)
    mixed = jnp.dot(active, w_out, preferred_element_type=jnp.float32) + b_out
    return (mixed, (normed, inv_std, lowered, slope, active))

def cell_backward(grad_mixed, saved, ln_gain, w_in, w_out):
    normed, inv_std, lowered, slope, active = saved
    grad_low = grad_mixed.astype(jnp.bfloat16)
    grad_wout = lax.dot_general(active, grad_low, (((0,), (0,)), ((), ())), preferred_element_type=jnp.float32)
    grad_act = lax.dot_general(grad_low, w_out, (((1,), (1,)), ((), ())), preferred_element_type=jnp.float32)
    grad_hid = (grad_act * slope).astype(jnp.bfloat16)
    grad_win = lax.dot_general(lowered, grad_hid, (((0,), (0,)), ((), ())), preferred_element_type=jnp.float32)
    grad_norm = lax.dot_general(grad_hid, w_in, (((1,), (1,)), ((), ())), preferred_element_type=jnp.float32) * ln_gain
    mean_one = lax.optimization_barrier(jnp.mean(grad_norm, axis=-1, keepdims=True))
    mean_two = lax.optimization_barrier(jnp.mean(grad_norm * normed, axis=-1, keepdims=True))
    grad_z = inv_std * (grad_norm - mean_one - normed * mean_two)
    return (grad_z, grad_win, grad_wout)

def pad_grid(field, partner):
    ext_cols = (jnp.arange(NLON + 6, dtype=jnp.int32) - 3) % NLON
    fold_cols = jnp.take(partner, ext_cols)
    wrapped = jnp.concatenate([field[:, NLON - 3:], field, field[:, :3]], axis=1)
    north = jnp.take(field[NLAT - 3:][::-1], fold_cols, axis=1)
    south = jnp.zeros((3, NLON + 6, field.shape[2]), field.dtype)
    return (jnp.concatenate([south, wrapped, north], axis=0), fold_cols)

def depthwise(padded, kernel, rows, cols):
    total = jnp.zeros((rows, cols, padded.shape[2]), jnp.float32)
    for row_off in range(7):
        for col_off in range(7):
            total = total + kernel[row_off, col_off] * padded[row_off:row_off + rows, col_off:col_off + cols].astype(jnp.float32)
    return total

def reference(states, grad_out, land_mask, partner, dw_kernel, dw_bias, ln_gain, ln_bias, w_in, b_in, w_out, b_out, layer_scale):
    masks = land_mask.astype(jnp.float32)
    padded_a, fold_cols = pad_grid(states[0], partner)
    padded_b, unused = pad_grid(states[1], partner)
    depth_a = depthwise(padded_a, dw_kernel, NLAT, NLON) + dw_bias
    depth_b = depthwise(padded_b, dw_kernel, NLAT, NLON) + dw_bias

    def forward_row(row):
        depth_row, field_row, mask_row = row
        mixed, saved = cell_forward(depth_row, ln_gain, ln_bias, w_in, b_in, w_out, b_out)
        return (field_row.astype(jnp.float32) + mask_row[:, None] * (layer_scale * mixed)).astype(jnp.bfloat16)
    out_a = lax.map(forward_row, (depth_a, states[0], masks))

    def backward_row(carry, row):
        depth_row, cot_row, mask_row = row
        mixed, saved = cell_forward(depth_row, ln_gain, ln_bias, w_in, b_in, w_out, b_out)
        grad_mixed = mask_row[:, None] * (layer_scale * cot_row.astype(jnp.float32))
        grad_z, part_win, part_wout = cell_backward(grad_mixed, saved, ln_gain, w_in, w_out)
        return ((carry[0] + part_win, carry[1] + part_wout), grad_z)
    start = (jnp.zeros((CH, HID), jnp.float32), jnp.zeros((HID, CH), jnp.float32))
    sums, grad_z = lax.scan(backward_row, start, (depth_b, grad_out, masks))
    kernel_rows = []
    for row_off in range(7):
        kernel_rows.append(jnp.stack([lax.optimization_barrier(jnp.sum(padded_b[row_off:row_off + NLAT, col_off:col_off + NLON].astype(jnp.float32) * grad_z, axis=(0, 1))) for col_off in range(7)]))
    sum_kernel = jnp.stack(kernel_rows)
    zero_pad = jnp.pad(grad_z, ((6, 6), (6, 6), (0, 0)))
    grad_pad = jnp.zeros((NLAT + 6, NLON + 6, CH), jnp.float32)
    for row_off in range(7):
        for col_off in range(7):
            grad_pad = grad_pad + dw_kernel[row_off, col_off] * zero_pad[6 - row_off:12 - row_off + NLAT, 6 - col_off:12 - col_off + NLON]
    core = grad_pad[3:NLAT + 3]
    grid = core[:, 3:NLON + 3]
    grid = grid.at[:, :3].add(core[:, NLON + 3:])
    grid = grid.at[:, NLON - 3:].add(core[:, :3])
    folded = jnp.zeros((3, NLON, CH), jnp.float32).at[:, fold_cols].add(grad_pad[NLAT + 3:])
    grid = grid.at[NLAT - 3:].add(folded[::-1])
    grad_states = grad_out.astype(jnp.float32) + grid
    scale = 1.0 / math.sqrt(NLAT * NLON)
    return (out_a, grad_states, sum_kernel * scale, sums[0] * scale, sums[1] * scale)
```

```python
import functools
import math

import jax
import jax.numpy as jnp
from jax import lax
from jax.experimental import pallas as pl
from jax.experimental.pallas import tpu as pltpu
from jax.sharding import PartitionSpec as P

F32 = jnp.float32
BF16 = jnp.bfloat16
MESH = pl.DeviceIdType.MESH

ROWS = 16
COLS = 64
PROWS = 22
WIDE = 80
LO = 128
CH = 192
HID = 768
NLON = 2048
CELLS = ROWS * COLS
CHUNK = 256
PIECE = 80
HALF = 16 * PIECE
QUART = 4 * PIECE
WIN_AT, WOUT_AT, WHI_AT, KER_AT = 0, 1152, 1920, 2304

root_factor = math.sqrt(2.0 / math.pi)
cubic_coef = 0.044715
norm_eps = 1e-06
scale = 1.0 / math.sqrt(64 * NLON)

LAT_AT, LON_AT, FOLD1_AT, FOLD2_AT = 0, 2, 8, 13
FIELD = 21
S0_AT, S1_AT, S2_AT, S3_AT, G1_AT, G2_AT, G3_AT = 42, 43, 46, 49, 52, 55, 58
COPIES = 59


def dot(a, b, dims=((1,), (0,))):
    return lax.dot_general(a, b, (dims, ((), ())), preferred_element_type=F32)


def kernel(
    x_ref, go_ref, mask_ref, partner_ref, dw_ref, dwb_ref, g_ref, lb_ref, win_ref, bin_ref,
    wout_ref, bout_ref, ls_ref,
    outa_ref, gs_ref, gk_ref, gwin_ref, gwout_ref,
    pd, pz, xb, zb, sx, sz, rlx, rlz, rcx, rcz, fx1, fz1, vx, vz, fx2, fz2,
    dp, mb, kt, wa, wb, gw, gwo, flat, r0, hb, r1, q, r2, r3, ag, ssem, rsem,
):
    lon = lax.axis_index("lon")
    lat = lax.axis_index("lat")
    top = lat == 3
    xx, yh, zz = lon // 8, (lon // 4) % 2, lon % 4
    yl, core = lat // 2, lat % 2
    yy = yh * 2 + yl

    def lon_of(step):
        return (lon + step + 64) % 32

    mate = (lon, lat + 1 - 2 * core)

    def first_peer(k):
        far_x = ((xx + k) % 4) * 8 + yh * 4 + zz
        far_z = xx * 8 + yh * 4 + (zz + k) % 4
        return (jnp.where(core == 0, far_x, far_z), lat)

    def second_peer(k):
        far_x = ((xx + k) % 4) * 8 + yh * 4 + zz
        far_z = xx * 8 + yh * 4 + (zz + k) % 4
        return (jnp.where(core == 0, far_z, far_x), lat)

    def third_peer(k):
        far = (yy + k) % 4
        return (xx * 8 + (far // 2) * 4 + zz, (far % 2) * 2 + core)

    c1 = jnp.where(core == 0, xx, zz)
    c2 = jnp.where(core == 0, zz, xx)

    def remote(src, dst, i, peer):
        return pltpu.make_async_remote_copy(
            src_ref=src, dst_ref=dst, send_sem=ssem.at[i], recv_sem=rsem.at[i],
            device_id={"lon": peer[0], "lat": peer[1]}, device_id_type=MESH,
        )

    barrier = pltpu.get_barrier_semaphore()

    def greet(peer):
        pl.semaphore_signal(
            barrier, inc=1, device_id={"lon": peer[0], "lat": peer[1]}, device_id_type=MESH
        )

    greet(mate)
    for k in (1, 2, 3):
        greet(first_peer(k))
        greet(second_peer(k))
        greet(third_peer(k))
    for side in (-1, 1):
        greet((lon_of(side), lat))
    for dl in (-1, 1):
        @pl.when((lat + dl >= 0) & (lat + dl <= 3))
        def _():
            for side in (-1, 0, 1):
                greet((lon_of(side), lat + dl))

    @pl.when(top)
    def _():
        for k in range(1, 6):
            greet((lon_of(k), lat))
        for k in range(8):
            greet((lon_of(31 - 2 * lon + 4 * k), lat))

    def at(plane, row, col):
        return (plane * PROWS + row) * WIDE + col

    def spread(r, carry):
        a = x_ref[0, r].astype(F32)
        b = x_ref[1, r].astype(F32)
        mix = jnp.concatenate([a[:, LO:], b[:, LO:]], axis=1)
        for plane, v in enumerate((a[:, :LO], b[:, :LO], mix)):
            pd[pl.ds(pl.multiple_of(at(plane, 3 + r, 8), 8), COLS), :] = v
            xb[plane, r] = v.astype(BF16)
        return carry

    lax.fori_loop(0, ROWS, spread, 0)

    def pack(field, send, planes):
        for plane in range(planes):
            for k in range(3):
                send[0, plane, k] = field[pl.ds(at(plane, 3, 8 + k), ROWS, stride=WIDE), :].astype(BF16)
                send[1, plane, k] = field[pl.ds(at(plane, 3, 69 + k), ROWS, stride=WIDE), :].astype(BF16)

    pack(pd, sx, 3)

    def clear_south(field, planes):
        for plane in range(planes):
            field[pl.ds(at(plane, 0, 0), 3 * WIDE), :] = jnp.zeros((3 * WIDE, LO), F32)

    clear_south(pd, 3)
    clear_south(pz, 2)

    peers = 12 + jnp.where(lat > 0, 3, 0) + jnp.where(lat < 3, 3, 0) + jnp.where(top, 13, 0)
    pl.semaphore_wait(barrier, peers)

    def lat_copies(base, block, got):
        return (
            (lat < 3, remote(block.at[:, 13:16], got.at[0], base + LAT_AT, (lon, lat + 1))),
            (lat > 0, remote(block.at[:, 0:3], got.at[1], base + LAT_AT + 1, (lon, lat - 1))),
        )

    def lon_copies(base, send, got):
        found = []
        for side in range(2):
            for slot in range(3):
                dl = 1 - slot
                found.append((
                    (lat + dl >= 0) & (lat + dl <= 3),
                    remote(
                        send.at[1 - side], got.at[side, slot], base + LON_AT + 3 * side + slot,
                        (lon_of(1 - 2 * side), lat + dl),
                    ),
                ))
        return found

    def lon_arrives(slot):
        return (lat + slot - 1 >= 0) & (lat + slot - 1 <= 3)

    def fold1_copies(base, block, got):
        return [
            remote(block.at[:, 13:16], got.at[k], base + FOLD1_AT + k - 1, (lon_of(-k), lat))
            for k in range(1, 6)
        ]

    def fold2_copies(base, window, got):
        return [
            remote(window, got.at[k], base + FOLD2_AT + k, (lon_of(31 - 2 * lon + 4 * k), lat))
            for k in range(8)
        ]

    def start_halo(base, block, send, rl, rc, f1):
        for cond, copy in lon_copies(base, send, rc):
            pl.when(cond)(copy.start)
        for cond, copy in lat_copies(base, block, rl):
            pl.when(cond)(copy.start)

        @pl.when(top)
        def _():
            for copy in fold1_copies(base, block, f1):
                copy.start()

    def finish_halo(base, field, planes, block, send, rl, rc):
        lats = lat_copies(base, block, rl)
        for way, (arrives, row) in enumerate(((lat > 0, 0), (lat < 3, 19))):
            @pl.when(arrives)
            def _(way=way, row=row):
                lats[way][1].wait_recv()
                for plane in range(planes):
                    for r in range(3):
                        field[pl.ds(at(plane, row + r, 8), COLS), :] = rl[way, plane, r].astype(F32)
        lons = lon_copies(base, send, rc)
        for side in range(2):
            col = 5 if side == 0 else 72
            for slot in range(3):
                @pl.when(lon_arrives(slot))
                def _(side=side, slot=slot, col=col):
                    lons[3 * side + slot][1].wait_recv()
                    for plane in range(planes):
                        for k in range(3):
                            v = rc[side, slot, plane, k].astype(F32)
                            if slot == 1:
                                field[pl.ds(at(plane, 3, col + k), ROWS, stride=WIDE), :] = v
                            else:
                                for r in range(3):
                                    row = r if slot == 0 else 19 + r
                                    own = 13 + r if slot == 0 else r
                                    field[pl.ds(at(plane, row, col + k), 1), :] = v[own:own + 1]

    begin = lax.rem(partner_ref[0] + (NLON - 2), NLON)
    offset = lax.rem(begin, COLS)
    near = lax.rem(lax.div(begin, COLS), 4)
    far = lax.div(begin, 4 * COLS)

    def middle_fold(base, planes, block, f1, window, f2):
        for copy in fold1_copies(base, block, f1):
            copy.wait_recv()
        f1[0] = block[:, 13:16]
        slot_at = lax.broadcasted_iota(jnp.int32, (WIDE, 3 * COLS), 0)
        from_at = lax.broadcasted_iota(jnp.int32, (WIDE, 3 * COLS), 1)
        pick = jnp.where(from_at + slot_at == offset + 74, 1.0, 0.0).astype(BF16)
        for plane in range(planes):
            for r in range(3):
                three = jnp.concatenate([f1[near + c, plane, r] for c in range(3)], axis=0)
                window[plane, r] = dot(pick, three).astype(BF16)
        for copy in fold2_copies(base, window, f2):
            copy.start()

    def finish_fold(base, field, planes, window, f2):
        for copy in fold2_copies(base, window, f2):
            copy.wait_recv()
        for plane in range(planes):
            for k in range(3):
                field[pl.ds(at(plane, 19 + k, 0), WIDE), :] = f2[far, plane, 2 - k].astype(F32)

    def close_field(base, block, send, rl, rc, f1, window, f2):
        for cond, copy in lat_copies(base, block, rl):
            pl.when(cond)(copy.wait_send)
        for cond, copy in lon_copies(base, send, rc):
            pl.when(cond)(copy.wait_send)

        @pl.when(top)
        def _():
            for copy in fold1_copies(base, block, f1):
                copy.wait_send()
            for copy in fold2_copies(base, window, f2):
                copy.wait_send()

    start_halo(0, xb, sx, rlx, rcx, fx1)

    lane = lax.broadcasted_iota(jnp.int32, (1, LO), 1)
    upper = lane >= 64

    def table(a, carry):
        low, high = dw_ref[a][:, :LO], dw_ref[a][:, LO:]
        mix = jnp.concatenate([high, high], axis=1)
        rlow, rhigh = dw_ref[6 - a][:, :LO], dw_ref[6 - a][:, LO:]
        rmix = jnp.concatenate([rhigh, rhigh], axis=1)
        for b in range(7):
            for kind, (v, w) in enumerate(((low, rlow), (mix, rmix))):
                straight = jnp.broadcast_to(v[b:b + 1], (8, LO))
                turned = jnp.broadcast_to(w[6 - b:7 - b], (8, LO))
                kt[kind, a * 7 + b] = straight
                kt[2 + kind, a * 7 + b] = turned
                kt[4 + kind, a * 7 + b] = jnp.where(top, straight, turned)
        return carry

    lax.fori_loop(0, 7, table, 0)
    wa[0:192] = win_ref[...]
    wa[192:256] = jnp.zeros((64, HID), BF16)
    wb[0:128] = win_ref[0:128]
    wb[128:192] = jnp.zeros((64, HID), BF16)
    wb[192:256] = win_ref[128:192]
    eye = jnp.where(
        lax.broadcasted_iota(jnp.int32, (COLS, COLS), 0) == lax.broadcasted_iota(jnp.int32, (COLS, COLS), 1),
        1.0, 0.0,
    ).astype(BF16)
    mask_t = dot(eye, mask_ref[...].astype(F32).astype(BF16), ((1,), (1,))).astype(BF16)
    for r in range(ROWS):
        one = jnp.where(lax.broadcasted_iota(jnp.int32, (ROWS, LO), 0) == r, 1.0, 0.0).astype(BF16)
        mb[r * COLS:(r + 1) * COLS] = dot(mask_t, one)
    gw[...] = jnp.zeros_like(gw)
    gwo[...] = jnp.zeros_like(gwo)

    zero64 = jnp.zeros((1, 64), F32)

    def halves(ref, state):
        v = ref[...]
        high = v[:, LO:]
        parts = [high, zero64] if state == 0 else [zero64, high]
        return v[:, :LO], jnp.concatenate(parts, axis=1)

    def conv(field, plane, c, half, tab, tab_last):
        base = at(plane, 4 * c, 32 * half + 5)
        acc = [[jnp.zeros((8, LO), F32) for _ in range(4)] for _ in range(4)]
        for p in range(10):
            for b in range(7):
                use = tab_last if p >= 7 else tab
                ks = {r: kt[use, (p - r) * 7 + b] for r in range(4) if 0 <= p - r <= 6}
                for t in range(4):
                    v = field[pl.ds(base + p * WIDE + 8 * t + b, 8), :]
                    for r, kv in ks.items():
                        acc[r][t] = acc[r][t] + kv * v
        return acc

    def norm(c, state):
        here = pl.ds(pl.multiple_of(c * CHUNK, CHUNK), CHUNK)
        keep = upper if state == 1 else jnp.logical_not(upper)
        blo, bhi = halves(dwb_ref, state)
        glo, ghi = halves(g_ref, state)
        llo, lhi = halves(lb_ref, state)
        lo = dp[state, here] + blo
        hi = jnp.where(keep, dp[2, here] + bhi, 0.0)
        mean = jnp.sum(lo + hi, axis=1, keepdims=True) * (1.0 / CH)
        lo = lo - mean
        hi = jnp.where(keep, hi - mean, 0.0)
        inv = lax.rsqrt(jnp.sum(lo * lo + hi * hi, axis=1, keepdims=True) * (1.0 / CH) + norm_eps)
        nlo, nhi = lo * inv, hi * inv
        low = jnp.concatenate(
            [(nlo * glo + llo).astype(BF16), (nhi * ghi + lhi).astype(BF16)], axis=1
        )
        return low, nlo, nhi, inv, glo, ghi, keep

    def forward_chunk(c):
        low = norm(c, 0)[0]
        mixed = jnp.broadcast_to(bout_ref[...], (CHUNK, CH))
        for s in range(3):
            cut = slice(256 * s, 256 * s + 256)
            u = dot(low, wa[:, cut]) + bin_ref[:, cut]
            t = jnp.tanh(u * (root_factor + (root_factor * cubic_coef) * (u * u)))
            act = (u * (0.5 + 0.5 * t)).astype(BF16)
            mixed = mixed + dot(act, wout_ref[cut])
        mixed = mixed * ls_ref[...]
        here = pl.ds(pl.multiple_of(c * CHUNK, CHUNK), CHUNK)
        m = mb[here]
        mm = jnp.concatenate([m, m[:, :64]], axis=1)
        for r in range(4):
            cut = slice(64 * r, 64 * r + 64)
            outa_ref[4 * c + r] = (x_ref[0, 4 * c + r].astype(F32) + mm[cut] * mixed[cut]).astype(BF16)

    def backward_chunk(c):
        low, nlo, nhi, inv, glo, ghi, keep = norm(c, 1)
        here = pl.ds(pl.multiple_of(c * CHUNK, CHUNK), CHUNK)
        m = mb[here]
        mm = jnp.concatenate([m, m[:, :64]], axis=1)
        go = jnp.concatenate([go_ref[4 * c + r] for r in range(4)], axis=0).astype(F32)
        gl = (mm * (ls_ref[...] * go)).astype(BF16)
        gn = jnp.zeros((CHUNK, 256), F32)
        for s in range(3):
            cut = slice(256 * s, 256 * s + 256)
            u = dot(low, wb[:, cut]) + bin_ref[:, cut]
            u2 = u * u
            t = jnp.tanh(u * (root_factor + (root_factor * cubic_coef) * u2))
            half = 0.5 + 0.5 * t
            value = u * half
            slope = half + value * (1.0 - t) * (root_factor + (3.0 * root_factor * cubic_coef) * u2)
            act = value.astype(BF16)
            gwo[cut] += dot(act, gl, ((0,), (0,)))
            gh = (dot(gl, wout_ref[cut], ((1,), (1,))) * slope).astype(BF16)
            gw[:, cut] += dot(low, gh, ((0,), (0,)))
            gn = gn + dot(gh, wb[:, cut], ((1,), (1,)))
        nl, nh = gn[:, :LO] * glo, gn[:, LO:] * ghi
        one = jnp.sum(nl + nh, axis=1, keepdims=True) * (1.0 / CH)
        two = jnp.sum(nl * nlo + nh * nhi, axis=1, keepdims=True) * (1.0 / CH)
        zl = inv * (nl - one - nlo * two)
        zh = jnp.where(keep, inv * (nh - one - nhi * two), 0.0)
        for plane, v in enumerate((zl, zh)):
            for r in range(4):
                cut = slice(64 * r, 64 * r + 64)
                pz[pl.ds(pl.multiple_of(at(plane, 3 + 4 * c + r, 8), 8), COLS), :] = v[cut]
                zb[plane, 4 * c + r] = v[cut].astype(BF16)

    finish_halo(0, pd, 3, xb, sx, rlx, rcx)

    @pl.when(top)
    def _():
        middle_fold(0, 3, xb, fx1, vx, fx2)

    def first_pass(c, carry):
        @pl.when(top & (c == 3))
        def _():
            finish_fold(0, pd, 3, vx, fx2)

        def sweep(i, carry):
            plane, half = i // 2, i % 2
            kind = plane // 2
            acc = conv(pd, plane, c, half, kind, kind)
            for r in range(4):
                for t in range(4):
                    cell = pl.multiple_of(c * CHUNK + r * COLS + half * 32 + 8 * t, 8)
                    dp[plane, pl.ds(cell, 8)] = acc[r][t]
            return carry

        lax.fori_loop(0, 6, sweep, 0)
        backward_chunk(c)
        return carry

    lax.fori_loop(0, 4, first_pass, 0)

    pack(pz, sz, 2)
    start_halo(FIELD, zb, sz, rlz, rcz, fz1)

    for plane in range(2):
        for rows in ((0, 1, 2, 3), (4, 5, 6)):
            def add_row(i, acc, plane=plane, rows=rows):
                acc = list(acc)
                for t in range(8):
                    z = pz[pl.ds(pl.multiple_of(at(plane, 3 + i, 8 + 8 * t), 8), 8), :]
                    for n, a in enumerate(rows):
                        for b in range(7):
                            v = pd[pl.ds(at(1 + plane, i + a, 5 + 8 * t + b), 8), :]
                            acc[n * 7 + b] = acc[n * 7 + b] + v * z
                return tuple(acc)

            acc = lax.fori_loop(
                0, ROWS, add_row, tuple(jnp.zeros((8, LO), F32) for _ in range(7 * len(rows)))
            )
            for n, a in enumerate(rows):
                for b in range(7):
                    line = KER_AT + plane * 56 + a * 7 + b
                    flat[line:line + 1] = jnp.sum(acc[n * 7 + b], axis=0, keepdims=True)
        flat[KER_AT + plane * 56 + 49:KER_AT + plane * 56 + 56] = jnp.zeros((7, LO), F32)
    flat[KER_AT + 112:2560] = jnp.zeros((2560 - KER_AT - 112, LO), F32)

    for s in range(6):
        cut = slice(128 * s, 128 * s + 128)
        flat[WIN_AT + 192 * s:WIN_AT + 192 * s + 128] = gw[0:128, cut]
        flat[WIN_AT + 192 * s + 128:WIN_AT + 192 * s + 192] = gw[192:256, cut]
    flat[WOUT_AT:WOUT_AT + HID] = gwo[:, :LO]
    flat[WHI_AT:WHI_AT + 384] = jnp.concatenate([gwo[0:384, LO:], gwo[384:768, LO:]], axis=1)

    def half_at(which):
        return pl.ds(pl.multiple_of(which * HALF, 8), HALF)

    s0 = remote(flat.at[half_at(1 - core)], r0, S0_AT, mate)

    def s1(k):
        return remote(hb.at[(c1 + k) % 4], r1.at[k - 1], S1_AT + k - 1, first_peer(k))

    def s2(k):
        return remote(q.at[(c2 + k) % 4], r2.at[k - 1], S2_AT + k - 1, second_peer(k))

    def s3(k):
        return remote(r3.at[yy], r3.at[yy], S3_AT + k - 1, third_peer(k))

    def s3_from(k):
        return remote(r3.at[yy], r3.at[(yy + 4 - k) % 4], S3_AT + k - 1, third_peer(k))

    def g1(k):
        return remote(ag.at[core, c1, c2], ag.at[core, c1, c2], G1_AT + k - 1, second_peer(k))

    def g1_from(k):
        return remote(ag.at[core, c1, c2], ag.at[core, c1, (c2 + 4 - k) % 4], G1_AT + k - 1, second_peer(k))

    def g2(k):
        return remote(ag.at[core, c1], ag.at[core, c1], G2_AT + k - 1, first_peer(k))

    def g2_from(k):
        return remote(ag.at[core, c1], ag.at[core, (c1 + 4 - k) % 4], G2_AT + k - 1, first_peer(k))

    g3 = remote(ag.at[core], ag.at[core], G3_AT, mate)
    g3_from = remote(ag.at[core], ag.at[1 - core], G3_AT, mate)

    s0.start()

    def second_pass(step, carry):
        @pl.when(step == 1)
        def _():
            finish_halo(FIELD, pz, 2, zb, sz, rlz, rcz)
            s0.wait_recv()
            for i in range(4):
                part = pl.ds(pl.multiple_of(core * HALF + i * QUART, 8), QUART)
                total = flat[part] + r0[i * QUART:(i + 1) * QUART]
                flat[part] = total
                hb[i] = total.astype(BF16)
            for k in (1, 2, 3):
                s1(k).start()

        @pl.when((step == 1) & top)
        def _():
            middle_fold(FIELD, 2, zb, fz1, vz, fz2)

        @pl.when(step == 2)
        def _():
            for k in (1, 2, 3):
                s1(k).wait_recv()
            total = flat[pl.ds(pl.multiple_of(core * HALF + c1 * QUART, 8), QUART)]
            for k in range(3):
                total = total + r1[k].astype(F32)
            for i in range(4):
                q[i] = total[i * PIECE:(i + 1) * PIECE]
            for k in (1, 2, 3):
                s2(k).start()

        @pl.when(step == 3)
        def _():
            for k in (1, 2, 3):
                s2(k).wait_recv()
            r3[yy] = q[c2] + r2[0] + r2[1] + r2[2]
            for k in (1, 2, 3):
                s3(k).start()

        @pl.when(step == 4)
        def _():
            for k in (1, 2, 3):
                s3_from(k).wait_recv()
            ag[core, c1, c2] = ((r3[0] + r3[1] + r3[2] + r3[3]) * scale).astype(BF16)
            for k in (1, 2, 3):
                g1(k).start()

        @pl.when(step == 5)
        def _():
            for k in (1, 2, 3):
                g1_from(k).wait_recv()
            for k in (1, 2, 3):
                g2(k).start()

        @pl.when(step == 6)
        def _():
            for k in (1, 2, 3):
                g2_from(k).wait_recv()
            g3.start()

        @pl.when((step == 7) & top)
        def _():
            finish_fold(FIELD, pz, 2, vz, fz2)

        @pl.when(step < 4)
        def _():
            forward_chunk(step)

        @pl.when(step >= 4)
        def _():
            c = step - 4
            last = jnp.where(c == 3, 4, 2)

            def sweep(half, carry):
                at_col = pl.ds(pl.multiple_of(32 * half, 32), 32)
                acc_lo = conv(pz, 0, c, half, 2, last)
                for r in range(4):
                    low = jnp.concatenate(acc_lo[r], axis=0)
                    go = go_ref[4 * c + r, at_col, :].astype(F32)
                    gs_ref[4 * c + r, at_col, 0:LO] = low + go[:, :LO]
                acc_hi = conv(pz, 1, c, half, 3, last + 1)
                for r in range(4):
                    high = jnp.concatenate(acc_hi[r], axis=0)
                    go = go_ref[4 * c + r, at_col, :].astype(F32)
                    gs_ref[4 * c + r, at_col, LO:CH] = high[:, 64:] + go[:, LO:]
                return carry

            lax.fori_loop(0, 2, sweep, 0)

        return carry

    lax.fori_loop(0, 8, second_pass, 0)

    g3_from.wait_recv()

    def part_of(start, size):
        first, end = start // PIECE, -(-(start + size) // PIECE)
        found = [ag[i // 16, (i // 4) % 4, i % 4] for i in range(first, end)]
        return jnp.concatenate(found, axis=0)[start - first * PIECE:start - first * PIECE + size].astype(F32)

    for s in range(6):
        gwin_ref[:, 128 * s:128 * s + 128] = part_of(WIN_AT + 192 * s, 192)
    gwout_ref[:, 0:LO] = part_of(WOUT_AT, HID)
    both = part_of(WHI_AT, 384)
    gwout_ref[0:384, LO:CH] = both[:, :64]
    gwout_ref[384:768, LO:CH] = both[:, 64:]
    klow = part_of(KER_AT, 56)
    khigh = part_of(KER_AT + 56, 56)
    for a in range(7):
        gk_ref[a, :, 0:LO] = klow[7 * a:7 * a + 7]
        gk_ref[a, :, LO:CH] = khigh[7 * a:7 * a + 7, 64:]

    close_field(0, xb, sx, rlx, rcx, fx1, vx, fx2)
    close_field(FIELD, zb, sz, rlz, rcz, fz1, vz, fz2)
    s0.wait_send()
    for k in (1, 2, 3):
        s1(k).wait_send()
        s2(k).wait_send()
        s3(k).wait_send()
        g1(k).wait_send()
        g2(k).wait_send()
    g3.wait_send()


def shards(states, grad_out, land_mask, partner, dw_kernel, dw_bias, ln_gain, ln_bias, w_in, b_in,
           w_out, b_out, layer_scale):
    def row(v):
        return v.reshape(1, v.shape[0])

    vmem = pl.BlockSpec(memory_space=pltpu.VMEM)
    smem = pl.BlockSpec(memory_space=pltpu.SMEM)

    def buf(*shape, dtype=F32):
        return pltpu.VMEM(shape, dtype)

    scratch = [
        buf(3 * PROWS * WIDE, LO), buf(2 * PROWS * WIDE, LO),
        buf(3, ROWS, COLS, LO, dtype=BF16), buf(2, ROWS, COLS, LO, dtype=BF16),
        buf(2, 3, 3, ROWS, LO, dtype=BF16), buf(2, 2, 3, ROWS, LO, dtype=BF16),
        buf(2, 3, 3, COLS, LO, dtype=BF16), buf(2, 2, 3, COLS, LO, dtype=BF16),
        buf(2, 3, 3, 3, ROWS, LO, dtype=BF16), buf(2, 3, 2, 3, ROWS, LO, dtype=BF16),
        buf(6, 3, 3, COLS, LO, dtype=BF16), buf(6, 2, 3, COLS, LO, dtype=BF16),
        buf(3, 3, WIDE, LO, dtype=BF16), buf(2, 3, WIDE, LO, dtype=BF16),
        buf(8, 3, 3, WIDE, LO, dtype=BF16), buf(8, 2, 3, WIDE, LO, dtype=BF16),
        buf(3, CELLS, LO), buf(CELLS, LO), buf(6, 49, 8, LO),
        buf(256, HID, dtype=BF16), buf(256, HID, dtype=BF16),
        buf(256, HID), buf(HID, CH), buf(2 * HALF, LO),
        buf(HALF, LO), buf(4, QUART, LO, dtype=BF16), buf(3, QUART, LO, dtype=BF16),
        buf(4, PIECE, LO), buf(3, PIECE, LO), buf(4, PIECE, LO),
        buf(2, 4, 4, PIECE, LO, dtype=BF16),
        pltpu.SemaphoreType.DMA((COPIES,)), pltpu.SemaphoreType.DMA((COPIES,)),
    ]
    outs = (
        jax.ShapeDtypeStruct((ROWS, COLS, CH), BF16),
        jax.ShapeDtypeStruct((ROWS, COLS, CH), F32),
        jax.ShapeDtypeStruct((7, 7, CH), F32),
        jax.ShapeDtypeStruct((CH, HID), F32),
        jax.ShapeDtypeStruct((HID, CH), F32),
    )
    return pl.pallas_call(
        kernel,
        out_shape=outs,
        in_specs=[vmem, vmem, vmem, smem] + [vmem] * 9,
        out_specs=(vmem,) * 5,
        scratch_shapes=scratch,
        compiler_params=pltpu.CompilerParams(
            collective_id=0, has_side_effects=True, vmem_limit_bytes=56 * 1024 * 1024
        ),
        name="block",
    )(
        states, grad_out, land_mask, partner, dw_kernel, row(dw_bias), row(ln_gain), row(ln_bias),
        w_in, row(b_in), w_out, row(b_out), row(layer_scale),
    )


def solution(mesh):
    placed = (
        P(None, "lat", "lon", None), P("lat", "lon", None), P("lat", "lon"),
        P(), P(), P(), P(), P(), P(), P(), P(), P(), P(),
    )
    return jax.shard_map(
        shards,
        mesh=mesh,
        in_specs=placed,
        out_specs=(P("lat", "lon", None), P("lat", "lon", None), P(), P(), P()),
        check_vma=False,
    )
```

```python
import functools
import math

import jax
import jax.numpy as jnp
from jax import lax
from jax.experimental import pallas as pl
from jax.experimental.pallas import tpu as pltpu
from jax.sharding import PartitionSpec as P

F32 = jnp.float32
BF16 = jnp.bfloat16
MESH = pl.DeviceIdType.MESH

ROWS = 16
COLS = 64
PROWS = 22
WIDE = 80
LO = 128
CH = 192
HID = 768
NLON = 2048
CELLS = ROWS * COLS
CHUNK = 256
PIECE = 80
HALF = 16 * PIECE
QUART = 4 * PIECE
WIN_AT, WOUT_AT, KER_AT = 0, 1152, 2304

root_factor = math.sqrt(2.0 / math.pi)
cubic_coef = 0.044715
norm_eps = 1e-06
scale = 1.0 / math.sqrt(64 * NLON)

LAT_AT, LON_AT, FIELD = 0, 2, 8
FOLD_B, FOLD_A, FOLD_Z, ROUND = 16, 30, 44, 6
S0_AT, S1_AT, S3_AT, G1_AT, G3_AT = 58, 59, 74, 77, 92
COPIES = 93


def dot(a, b, dims=((1,), (0,))):
    return lax.dot_general(a, b, (dims, ((), ())), preferred_element_type=F32)


def kernel(
    x_in, go_in, mask_in, partner_in, dw_in, dwb_in, g_in, lb_in, win_in, bin_in,
    wout_in, bout_in, ls_in,
    outa_ref, gs_ref, gk_ref, gwin_ref, gwout_ref,
    x_ref, go_ref, mask_ref, partner_ref, dw_ref, dwb_ref, g_ref, lb_ref, win_ref, bin_ref,
    wout_ref, bout_ref, ls_ref, load_sem,
    pd, pz, xb, zb, sx, sz, rlx, rlz, rcx, rcz, fb1, fa1, fz1, vb, va, vz, fb2, fya, fyz, fxa, fxz,
    dp, mb, kt, wa, wb, gw, gwo, gka, flat, b0, r0, hb, r1, r3, ag, ssem, rsem,
):
    lon = lax.axis_index("lon")
    lat = lax.axis_index("lat")
    top = lat == 3
    xx, yh, zz = lon // 8, (lon // 4) % 2, lon % 4
    yl, core = lat // 2, lat % 2
    yy = yh * 2 + yl

    def lon_of(step):
        return (lon + step + 64) % 32

    mate = (lon, lat + 1 - 2 * core)

    def plane_peer(m):
        return (((xx + m // 4) % 4) * 8 + yh * 4 + (zz + m % 4) % 4, lat)

    def third_peer(k):
        far = (yy + k) % 4
        return (xx * 8 + (far // 2) * 4 + zz, (far % 2) * 2 + core)

    place = xx * 4 + zz

    def place_of(m):
        return ((xx + m // 4) % 4) * 4 + (zz + m % 4) % 4

    block8 = lon // 4
    mirror = lon + 3 - 2 * zz
    own1 = 2 * zz - 3
    own2 = (2 * block8 + 1) % 8

    def mirror_of(v):
        return v + 3 - 2 * (v % 4)

    def fold1_to(k):
        return mirror_of(lon_of(-k))

    def fold1_from(k):
        return (mirror + k) % 32

    def fold2_peer(k):
        return ((7 - block8 + k) % 8) * 4 + zz

    def remote(src, dst, i, peer):
        return pltpu.make_async_remote_copy(
            src_ref=src, dst_ref=dst, send_sem=ssem.at[i], recv_sem=rsem.at[i],
            device_id={"lon": peer[0], "lat": peer[1]}, device_id_type=MESH,
        )

    barrier = pltpu.get_barrier_semaphore()

    def greet(peer):
        pl.semaphore_signal(
            barrier, inc=1, device_id={"lon": peer[0], "lat": peer[1]}, device_id_type=MESH
        )

    greet(mate)
    for m in range(1, 16):
        greet(plane_peer(m))
    for k in (1, 2, 3):
        greet(third_peer(k))
    for side in (-1, 1):
        greet((lon_of(side), lat))
    for dl in (-1, 1):
        @pl.when((lat + dl >= 0) & (lat + dl <= 3))
        def _():
            for side in (-1, 0, 1):
                greet((lon_of(side), lat + dl))

    @pl.when(top)
    def _():
        for k in range(6):
            @pl.when(k != own1)
            def _(k=k):
                greet((fold1_from(k), lat))
        for k in range(8):
            @pl.when(k != own2)
            def _(k=k):
                greet((fold2_peer(k), lat))

    ins = (x_in, go_in, mask_in, partner_in, dw_in, dwb_in, g_in, lb_in, win_in, bin_in,
           wout_in, bout_in, ls_in)
    held = (x_ref, go_ref, mask_ref, partner_ref, dw_ref, dwb_ref, g_ref, lb_ref, win_ref, bin_ref,
            wout_ref, bout_ref, ls_ref)
    loads = [pltpu.make_async_copy(a, b, load_sem.at[i]) for i, (a, b) in enumerate(zip(ins, held))]
    for load in loads:
        load.start()
    loads[0].wait()

    def at(plane, row, col):
        return (plane * PROWS + row) * WIDE + col

    def spread(r, carry):
        a = x_ref[0, r].astype(F32)
        b = x_ref[1, r].astype(F32)
        mix = jnp.concatenate([a[:, LO:], b[:, LO:]], axis=1)
        for plane, v in enumerate((a[:, :LO], b[:, :LO], mix)):
            pd[pl.ds(pl.multiple_of(at(plane, 3 + r, 8), 8), COLS), :] = v
            xb[plane, r] = v.astype(BF16)
        return carry

    lax.fori_loop(0, ROWS, spread, 0)

    def pack(field, send, planes):
        for plane in range(planes):
            for k in range(3):
                send[0, plane, k] = field[pl.ds(at(plane, 3, 8 + k), ROWS, stride=WIDE), :].astype(BF16)
                send[1, plane, k] = field[pl.ds(at(plane, 3, 69 + k), ROWS, stride=WIDE), :].astype(BF16)

    pack(pd, sx, 3)

    peers = 21 + jnp.where(lat > 0, 3, 0) + jnp.where(lat < 3, 3, 0)
    peers = peers + jnp.where(top, 13 - jnp.where(zz >= 2, 1, 0), 0)
    pl.semaphore_wait(barrier, peers)

    def lat_copies(base, block, got):
        return (
            (lat < 3, remote(block.at[:, 13:16], got.at[0], base + LAT_AT, (lon, lat + 1))),
            (lat > 0, remote(block.at[:, 0:3], got.at[1], base + LAT_AT + 1, (lon, lat - 1))),
        )

    def lon_copies(base, send, got):
        found = []
        for side in range(2):
            for slot in range(3):
                dl = 1 - slot
                found.append((
                    (lat + dl >= 0) & (lat + dl <= 3),
                    remote(
                        send.at[1 - side], got.at[side, slot], base + LON_AT + 3 * side + slot,
                        (lon_of(1 - 2 * side), lat + dl),
                    ),
                ))
        return found

    def lon_arrives(slot):
        return (lat + slot - 1 >= 0) & (lat + slot - 1 <= 3)

    def fold1_copies(base, block, planes, got):
        found = []
        for k in range(6):
            width = 16 if k == 5 else COLS
            found.append((k != own1, remote(
                block.at[planes, 13:16, 0:width], got.at[k, :, :, 0:width], base + k,
                (fold1_to(k), lat),
            )))
        return found

    def fold2_copies(base, window, got):
        return [
            (k != own2, remote(window, got.at[k], base + ROUND + k, (fold2_peer(k), lat)))
            for k in range(8)
        ]

    def start_fold(base, block, planes, f1):
        for cond, copy in fold1_copies(base, block, planes, f1):
            pl.when(cond)(copy.start)

    def start_halo(base, block, send, rl, rc):
        for cond, copy in lon_copies(base, send, rc):
            pl.when(cond)(copy.start)
        for cond, copy in lat_copies(base, block, rl):
            pl.when(cond)(copy.start)

    def finish_halo(base, field, planes, block, send, rl, rc):
        lats = lat_copies(base, block, rl)
        for way, (arrives, row) in enumerate(((lat > 0, 0), (lat < 3, 19))):
            @pl.when(arrives)
            def _(way=way, row=row):
                lats[way][1].wait_recv()
                for plane in range(planes):
                    for r in range(3):
                        field[pl.ds(at(plane, row + r, 8), COLS), :] = rl[way, plane, r].astype(F32)
        lons = lon_copies(base, send, rc)
        for side in range(2):
            col = 5 if side == 0 else 72
            for slot in range(3):
                @pl.when(lon_arrives(slot))
                def _(side=side, slot=slot, col=col):
                    lons[3 * side + slot][1].wait_recv()
                    for plane in range(planes):
                        for k in range(3):
                            v = rc[side, slot, plane, k].astype(F32)
                            if slot == 1:
                                field[pl.ds(at(plane, 3, col + k), ROWS, stride=WIDE), :] = v
                            else:
                                for r in range(3):
                                    row = r if slot == 0 else 19 + r
                                    own = 13 + r if slot == 0 else r
                                    field[pl.ds(at(plane, row, col + k), 1), :] = v[own:own + 1]

    def shift_parts():
        begin = lax.rem(partner_ref[0] + (NLON - 2), NLON)
        return lax.rem(begin, COLS), lax.rem(lax.div(begin, COLS), 4), lax.div(begin, 4 * COLS)

    def make_window(base, block, planes, f1, window):
        offset, near, _ = shift_parts()
        for cond, copy in fold1_copies(base, block, planes, f1):
            pl.when(cond)(copy.wait_recv)

        @pl.when(zz >= 2)
        def _():
            f1[own1] = block[planes, 13:16]

        slot_at = lax.broadcasted_iota(jnp.int32, (WIDE, 3 * COLS), 0)
        from_at = lax.broadcasted_iota(jnp.int32, (WIDE, 3 * COLS), 1)
        pick = jnp.where(from_at + slot_at == offset + 74, 1.0, 0.0).astype(BF16)
        for plane in range(window.shape[0]):
            for r in range(3):
                three = jnp.concatenate([f1[near + c, plane, r] for c in range(3)], axis=0)
                window[plane, r] = dot(pick, three).astype(BF16)

    def middle_fold(base, block, planes, f1, window, f2):
        make_window(base, block, planes, f1, window)
        for cond, copy in fold2_copies(base, window, f2):
            pl.when(cond)(copy.start)
        f2[own2] = window[...]

    def foldy_copy(base, window, fy):
        return remote(window, fy.at[yh], base + ROUND, (xx * 8 + (1 - yh) * 4 + zz, lat))

    def foldy_from(base, window, fy):
        return remote(window, fy.at[1 - yh], base + ROUND, (xx * 8 + (1 - yh) * 4 + zz, lat))

    def foldx_copies(base, fy, fx):
        return [
            remote(fy.at[2], fx.at[xx], base + ROUND + k, (((xx + k) % 4) * 8 + yh * 4 + zz, lat))
            for k in (1, 2, 3)
        ]

    def foldx_from(base, fy, fx):
        return [
            remote(fy.at[2], fx.at[(xx + 4 - k) % 4], base + ROUND + k, (((xx + k) % 4) * 8 + yh * 4 + zz, lat))
            for k in (1, 2, 3)
        ]

    def fold_to_y(base, block, planes, f1, window, fy):
        make_window(base, block, planes, f1, window)
        foldy_copy(base, window, fy).start()
        fy[yh] = window[...]

    def fold_to_x(base, window, fy, fx):
        foldy_from(base, window, fy).wait_recv()
        far = shift_parts()[2]
        chosen = fy[lax.rem(1 - yh + far, 2)]
        fy[2] = chosen
        for copy in foldx_copies(base, fy, fx):
            copy.start()
        fx[xx] = chosen

    def end_fold(base, field, first, fy, fx):
        for copy in foldx_from(base, fy, fx):
            copy.wait_recv()
        far = shift_parts()[2]
        source = lax.div(lax.rem(7 - block8 + far, 8), 2)
        for plane in range(fx.shape[1]):
            for k in range(3):
                field[pl.ds(at(first + plane, 19 + k, 0), WIDE), :] = fx[source, plane, 2 - k].astype(F32)

    def close_three(base, block, planes, f1, window, fy, fx):
        for cond, copy in fold1_copies(base, block, planes, f1):
            pl.when(cond)(copy.wait_send)
        foldy_copy(base, window, fy).wait_send()
        for copy in foldx_copies(base, fy, fx):
            copy.wait_send()

    def finish_fold(base, field, first, window, f2):
        for cond, copy in fold2_copies(base, window, f2):
            pl.when(cond)(copy.wait_recv)
        far = shift_parts()[2]
        for plane in range(window.shape[0]):
            for k in range(3):
                field[pl.ds(at(first + plane, 19 + k, 0), WIDE), :] = f2[far, plane, 2 - k].astype(F32)

    def close_fold(base, block, planes, f1, window, f2):
        for cond, copy in fold1_copies(base, block, planes, f1):
            pl.when(cond)(copy.wait_send)
        for cond, copy in fold2_copies(base, window, f2):
            pl.when(cond)(copy.wait_send)

    def close_field(base, block, send, rl, rc):
        for cond, copy in lat_copies(base, block, rl):
            pl.when(cond)(copy.wait_send)
        for cond, copy in lon_copies(base, send, rc):
            pl.when(cond)(copy.wait_send)

    in_b, in_a, in_z = slice(1, 3), slice(0, 1), slice(0, 2)

    @pl.when(top)
    def _():
        start_fold(FOLD_B, xb, in_b, fb1)

    start_halo(0, xb, sx, rlx, rcx)

    for load in loads[1:]:
        load.wait()

    def clear_south(field, planes):
        for plane in range(planes):
            field[pl.ds(at(plane, 0, 0), 3 * WIDE), :] = jnp.zeros((3 * WIDE, LO), F32)

    clear_south(pd, 3)
    clear_south(pz, 2)

    lane = lax.broadcasted_iota(jnp.int32, (1, LO), 1)
    upper = lane >= 64

    def table(a, carry):
        low, high = dw_ref[a][:, :LO], dw_ref[a][:, LO:]
        mix = jnp.concatenate([high, high], axis=1)
        rlow, rhigh = dw_ref[6 - a][:, :LO], dw_ref[6 - a][:, LO:]
        rmix = jnp.concatenate([rhigh, rhigh], axis=1)
        for b in range(7):
            for kind, (v, w) in enumerate(((low, rlow), (mix, rmix))):
                straight = jnp.broadcast_to(v[b:b + 1], (8, LO))
                turned = jnp.broadcast_to(w[6 - b:7 - b], (8, LO))
                kt[kind, a * 7 + b] = straight
                kt[2 + kind, a * 7 + b] = turned
                kt[4 + kind, a * 7 + b] = jnp.where(top, straight, turned)
        return carry

    lax.fori_loop(0, 7, table, 0)
    wa[0:192] = win_ref[...]
    wa[192:256] = jnp.zeros((64, HID), BF16)
    wb[0:128] = win_ref[0:128]
    wb[128:192] = jnp.zeros((64, HID), BF16)
    wb[192:256] = win_ref[128:192]
    eye = jnp.where(
        lax.broadcasted_iota(jnp.int32, (COLS, COLS), 0) == lax.broadcasted_iota(jnp.int32, (COLS, COLS), 1),
        1.0, 0.0,
    ).astype(BF16)
    mask_t = dot(eye, mask_ref[...].astype(F32).astype(BF16), ((1,), (1,))).astype(BF16)
    for r in range(ROWS):
        one = jnp.where(lax.broadcasted_iota(jnp.int32, (ROWS, LO), 0) == r, 1.0, 0.0).astype(BF16)
        mb[r * COLS:(r + 1) * COLS] = dot(mask_t, one)
    gw[...] = jnp.zeros_like(gw)
    gwo[...] = jnp.zeros_like(gwo)
    gka[...] = jnp.zeros_like(gka)
    flat[KER_AT:2560] = jnp.zeros((2560 - KER_AT, LO), F32)
    for f1 in (fb1, fa1, fz1):
        f1[5, :, :, 16:64] = jnp.zeros_like(f1[5, :, :, 16:64])


    zero64 = jnp.zeros((1, 64), F32)

    def halves(ref, state):
        v = ref[...]
        high = v[:, LO:]
        parts = [high, zero64] if state == 0 else [zero64, high]
        return v[:, :LO], jnp.concatenate(parts, axis=1)

    def conv(field, plane, c, half, tab, tab_last):
        base = at(plane, 4 * c, 32 * half + 5)
        acc = [[jnp.zeros((8, LO), F32) for _ in range(4)] for _ in range(4)]
        for p in range(10):
            for b in range(7):
                use = tab_last if p >= 7 else tab
                ks = {r: kt[use, (p - r) * 7 + b] for r in range(4) if 0 <= p - r <= 6}
                for t in range(4):
                    v = field[pl.ds(base + p * WIDE + 8 * t + b, 8), :]
                    for r, kv in ks.items():
                        acc[r][t] = acc[r][t] + kv * v
        return acc

    def bias(s):
        return jnp.concatenate([bin_ref[2 * s:2 * s + 1], bin_ref[2 * s + 1:2 * s + 2]], axis=1)

    def norm(c, state):
        here = pl.ds(pl.multiple_of(c * CHUNK, CHUNK), CHUNK)
        keep = upper if state == 1 else jnp.logical_not(upper)
        blo, bhi = halves(dwb_ref, state)
        glo, ghi = halves(g_ref, state)
        llo, lhi = halves(lb_ref, state)
        lo = dp[state, here] + blo
        hi = jnp.where(keep, dp[2, here] + bhi, 0.0)
        mean = jnp.sum(lo + hi, axis=1, keepdims=True) * (1.0 / CH)
        lo = lo - mean
        hi = jnp.where(keep, hi - mean, 0.0)
        inv = lax.rsqrt(jnp.sum(lo * lo + hi * hi, axis=1, keepdims=True) * (1.0 / CH) + norm_eps)
        nlo, nhi = lo * inv, hi * inv
        low = jnp.concatenate(
            [(nlo * glo + llo).astype(BF16), (nhi * ghi + lhi).astype(BF16)], axis=1
        )
        return low, nlo, nhi, inv, glo, ghi, keep

    def forward_chunk(c):
        low = norm(c, 0)[0]
        mixed = jnp.broadcast_to(bout_ref[...], (CHUNK, CH))
        for s in range(3):
            cut = slice(256 * s, 256 * s + 256)
            u = dot(low, wa[:, cut]) + bias(s)
            t = jnp.tanh(u * (root_factor + (root_factor * cubic_coef) * (u * u)))
            act = (u * (0.5 + 0.5 * t)).astype(BF16)
            mixed = mixed + dot(act, wout_ref[:, cut], ((1,), (1,)))
        mixed = mixed * ls_ref[...]
        here = pl.ds(pl.multiple_of(c * CHUNK, CHUNK), CHUNK)
        m = mb[here]
        mm = jnp.concatenate([m, m[:, :64]], axis=1)
        for r in range(4):
            cut = slice(64 * r, 64 * r + 64)
            outa_ref[4 * c + r] = (x_ref[0, 4 * c + r].astype(F32) + mm[cut] * mixed[cut]).astype(BF16)

    def backward_chunk(c):
        low, nlo, nhi, inv, glo, ghi, keep = norm(c, 1)
        here = pl.ds(pl.multiple_of(c * CHUNK, CHUNK), CHUNK)
        m = mb[here]
        mm = jnp.concatenate([m, m[:, :64]], axis=1)
        go = jnp.concatenate([go_ref[4 * c + r] for r in range(4)], axis=0).astype(F32)
        gl = (mm * (ls_ref[...] * go)).astype(BF16)
        gn = jnp.zeros((CHUNK, 256), F32)
        for s in range(3):
            cut = slice(256 * s, 256 * s + 256)
            u = dot(low, wb[:, cut]) + bias(s)
            u2 = u * u
            t = jnp.tanh(u * (root_factor + (root_factor * cubic_coef) * u2))
            half = 0.5 + 0.5 * t
            value = u * half
            slope = half + value * (1.0 - t) * (root_factor + (3.0 * root_factor * cubic_coef) * u2)
            act = value.astype(BF16)
            gwo[:, cut] += dot(gl, act, ((0,), (0,)))
            gh = (dot(gl, wout_ref[:, cut]) * slope).astype(BF16)
            gw[:, cut] += dot(low, gh, ((0,), (0,)))
            gn = gn + dot(gh, wb[:, cut], ((1,), (1,)))
        nl, nh = gn[:, :LO] * glo, gn[:, LO:] * ghi
        one = jnp.sum(nl + nh, axis=1, keepdims=True) * (1.0 / CH)
        two = jnp.sum(nl * nlo + nh * nhi, axis=1, keepdims=True) * (1.0 / CH)
        zl = inv * (nl - one - nlo * two)
        zh = jnp.where(keep, inv * (nh - one - nhi * two), 0.0)
        for plane, v in enumerate((zl, zh)):
            for r in range(4):
                cut = slice(64 * r, 64 * r + 64)
                pz[pl.ds(pl.multiple_of(at(plane, 3 + 4 * c + r, 8), 8), COLS), :] = v[cut]
                zb[plane, 4 * c + r] = v[cut].astype(BF16)

    def sweep_states(plane, c):
        def sweep(half, carry):
            kind = plane // 2
            acc = conv(pd, plane, c, half, kind, kind)
            for r in range(4):
                for t in range(4):
                    cell = pl.multiple_of(c * CHUNK + r * COLS + half * 32 + 8 * t, 8)
                    dp[plane, pl.ds(cell, 8)] = acc[r][t]
            return carry

        lax.fori_loop(0, 2, sweep, 0)

    def kernel_chunk(c):
        for plane in range(2):
            for rows in ((0, 1, 2, 3), (4, 5, 6)):
                def add_row(i, acc, plane=plane, rows=rows):
                    acc = list(acc)
                    for t in range(8):
                        z = pz[pl.ds(pl.multiple_of(at(plane, 3 + i, 8 + 8 * t), 8), 8), :]
                        for n, a in enumerate(rows):
                            for b in range(7):
                                v = pd[pl.ds(at(1 + plane, i + a, 5 + 8 * t + b), 8), :]
                                acc[n * 7 + b] = acc[n * 7 + b] + v * z
                    return tuple(acc)

                acc = lax.fori_loop(
                    4 * c, 4 * c + 4, add_row,
                    tuple(jnp.zeros((8, LO), F32) for _ in range(7 * len(rows))),
                )
                for n, a in enumerate(rows):
                    for b in range(7):
                        gka[plane, a * 7 + b] += acc[n * 7 + b]

    finish_halo(0, pd, 3, xb, sx, rlx, rcx)

    def first_pass(c, carry):
        @pl.when(top & (c == 2))
        def _():
            fold_to_y(FOLD_A, xb, in_a, fa1, va, fya)

        @pl.when(top & (c == 3))
        def _():
            finish_fold(FOLD_B, pd, 1, vb, fb2)
            fold_to_x(FOLD_A, va, fya, fxa)

        def both(plane, carry):
            sweep_states(plane, c)
            return carry

        lax.fori_loop(1, 3, both, 0)

        @pl.when(top & (c == 0))
        def _():
            middle_fold(FOLD_B, xb, in_b, fb1, vb, fb2)
            start_fold(FOLD_A, xb, in_a, fa1)

        backward_chunk(c)
        kernel_chunk(c)
        return carry

    lax.fori_loop(0, 4, first_pass, 0)

    for plane in range(2):
        for n in range(49):
            line = KER_AT + plane * 56 + n
            flat[line:line + 1] = jnp.sum(gka[plane, n], axis=0, keepdims=True)

    for s in range(6):
        cut = slice(128 * s, 128 * s + 128)
        flat[WIN_AT + 192 * s:WIN_AT + 192 * s + 128] = gw[0:128, cut]
        flat[WIN_AT + 192 * s + 128:WIN_AT + 192 * s + 192] = gw[192:256, cut]
        flat[WOUT_AT + 192 * s:WOUT_AT + 192 * s + 192] = gwo[:, cut]

    def half_at(which):
        return pl.ds(pl.multiple_of(which * HALF, 8), HALF)

    b0[...] = flat[half_at(1 - core)].astype(BF16)
    s0 = remote(b0, r0, S0_AT, mate)

    def s1(m):
        return remote(hb.at[place_of(m)], r1.at[m - 1], S1_AT + m - 1, plane_peer(m))

    def s3(k):
        return remote(r3.at[yy], r3.at[yy], S3_AT + k - 1, third_peer(k))

    def s3_from(k):
        return remote(r3.at[yy], r3.at[(yy + 4 - k) % 4], S3_AT + k - 1, third_peer(k))

    def g1(m):
        return remote(ag.at[core, place], ag.at[core, place], G1_AT + m - 1, plane_peer(m))

    def g1_from(m):
        there = ((xx + 4 - m // 4) % 4) * 4 + (zz + 4 - m % 4) % 4
        return remote(ag.at[core, place], ag.at[core, there], G1_AT + m - 1, plane_peer(m))

    g3 = remote(ag.at[core], ag.at[core], G3_AT, mate)
    g3_from = remote(ag.at[core], ag.at[1 - core], G3_AT, mate)

    s0.start()

    pack(pz, sz, 2)

    @pl.when(top)
    def _():
        start_fold(FOLD_Z, zb, in_z, fz1)

    start_halo(FIELD, zb, sz, rlz, rcz)

    def second_pass(c, carry):
        @pl.when(c == 1)
        def _():
            s0.wait_recv()
            for i in range(16):
                part = pl.ds(pl.multiple_of(core * HALF + i * PIECE, 8), PIECE)
                total = flat[part] + r0[i * PIECE:(i + 1) * PIECE].astype(F32)
                flat[part] = total
                hb[i] = total.astype(BF16)
            for m in range(1, 16):
                s1(m).start()

        @pl.when(top & (c == 3))
        def _():
            end_fold(FOLD_A, pd, 0, fya, fxa)

        sweep_states(0, c)
        forward_chunk(c)
        return carry

    lax.fori_loop(0, 4, second_pass, 0)

    finish_halo(FIELD, pz, 2, zb, sz, rlz, rcz)

    @pl.when(top)
    def _():
        fold_to_y(FOLD_Z, zb, in_z, fz1, vz, fyz)

    def third_pass(c, carry):
        @pl.when(c == 1)
        def _():
            for m in range(1, 16):
                s1(m).wait_recv()
            total = flat[pl.ds(pl.multiple_of(core * HALF + place * PIECE, 8), PIECE)]
            for m in range(15):
                total = total + r1[m].astype(F32)
            r3[yy] = total
            for k in (1, 2, 3):
                s3(k).start()

        @pl.when(top & (c == 2))
        def _():
            fold_to_x(FOLD_Z, vz, fyz, fxz)

        @pl.when(c == 3)
        def _():
            for k in (1, 2, 3):
                s3_from(k).wait_recv()
            ag[core, place] = ((r3[0] + r3[1] + r3[2] + r3[3]) * scale).astype(BF16)
            for m in range(1, 16):
                g1(m).start()

        @pl.when(top & (c == 3))
        def _():
            end_fold(FOLD_Z, pz, 0, fyz, fxz)

        last = jnp.where(c == 3, 4, 2)

        def sweep(half, carry):
            at_col = pl.ds(pl.multiple_of(32 * half, 32), 32)
            acc_lo = conv(pz, 0, c, half, 2, last)
            for r in range(4):
                low = jnp.concatenate(acc_lo[r], axis=0)
                go = go_ref[4 * c + r, at_col, :].astype(F32)
                gs_ref[4 * c + r, at_col, 0:LO] = low + go[:, :LO]
            acc_hi = conv(pz, 1, c, half, 3, last + 1)
            for r in range(4):
                high = jnp.concatenate(acc_hi[r], axis=0)
                go = go_ref[4 * c + r, at_col, :].astype(F32)
                gs_ref[4 * c + r, at_col, LO:CH] = high[:, 64:] + go[:, LO:]
            return carry

        lax.fori_loop(0, 2, sweep, 0)
        return carry

    lax.fori_loop(0, 4, third_pass, 0)

    for m in range(1, 16):
        g1_from(m).wait_recv()
    g3.start()
    g3_from.wait_recv()

    def part_of(start, size):
        first, end = start // PIECE, -(-(start + size) // PIECE)
        found = [ag[i // 16, i % 16] for i in range(first, end)]
        return jnp.concatenate(found, axis=0)[start - first * PIECE:start - first * PIECE + size].astype(F32)

    for s in range(6):
        gwin_ref[:, 128 * s:128 * s + 128] = part_of(WIN_AT + 192 * s, 192)
        gwout_ref[:, 128 * s:128 * s + 128] = part_of(WOUT_AT + 192 * s, 192)
    klow = part_of(KER_AT, 56)
    khigh = part_of(KER_AT + 56, 56)
    for a in range(7):
        gk_ref[a, :, 0:LO] = klow[7 * a:7 * a + 7]
        gk_ref[a, :, LO:CH] = khigh[7 * a:7 * a + 7, 64:]

    close_field(0, xb, sx, rlx, rcx)
    close_field(FIELD, zb, sz, rlz, rcz)

    @pl.when(top)
    def _():
        close_fold(FOLD_B, xb, in_b, fb1, vb, fb2)
        close_three(FOLD_A, xb, in_a, fa1, va, fya, fxa)
        close_three(FOLD_Z, zb, in_z, fz1, vz, fyz, fxz)

    s0.wait_send()
    for m in range(1, 16):
        s1(m).wait_send()
        g1(m).wait_send()
    for k in (1, 2, 3):
        s3(k).wait_send()
    g3.wait_send()


def move(*refs):
    count = (len(refs) - 2) // 3
    ins, outs, held = refs[:count], refs[count:2 * count], refs[2 * count:3 * count]
    come, go = refs[-2:]
    first = [pltpu.make_async_copy(ins[i], held[i], come.at[i]) for i in range(count)]
    second = [pltpu.make_async_copy(held[i], outs[i], go.at[i]) for i in range(count)]
    for copy in first:
        copy.start()
    for i in range(count):
        first[i].wait()
        second[i].start()
    for copy in second:
        copy.wait()


def shards(states, grad_out, land_mask, partner, dw_kernel, dw_bias, ln_gain, ln_bias, w_in, b_in,
           w_out, b_out, layer_scale):
    def row(v):
        return v.reshape(1, v.shape[0])

    vmem = pl.BlockSpec(memory_space=pltpu.VMEM)
    anywhere = pl.BlockSpec(memory_space=pl.ANY)

    def buf(*shape, dtype=F32):
        return pltpu.VMEM(shape, dtype)

    load_to = [
        buf(2, ROWS, COLS, CH, dtype=BF16), buf(ROWS, COLS, CH, dtype=BF16),
        buf(ROWS, COLS, dtype=jnp.int32), pltpu.SMEM((NLON,), jnp.int32), buf(7, 7, CH),
        buf(1, CH), buf(1, CH), buf(1, CH), buf(CH, HID, dtype=BF16), buf(HID // LO, LO),
        buf(CH, HID, dtype=BF16), buf(1, CH), buf(1, CH), pltpu.SemaphoreType.DMA((13,)),
    ]
    scratch = load_to + [
        buf(3 * PROWS * WIDE, LO), buf(2 * PROWS * WIDE, LO),
        buf(3, ROWS, COLS, LO, dtype=BF16), buf(2, ROWS, COLS, LO, dtype=BF16),
        buf(2, 3, 3, ROWS, LO, dtype=BF16), buf(2, 2, 3, ROWS, LO, dtype=BF16),
        buf(2, 3, 3, COLS, LO, dtype=BF16), buf(2, 2, 3, COLS, LO, dtype=BF16),
        buf(2, 3, 3, 3, ROWS, LO, dtype=BF16), buf(2, 3, 2, 3, ROWS, LO, dtype=BF16),
        buf(6, 2, 3, COLS, LO, dtype=BF16), buf(6, 1, 3, COLS, LO, dtype=BF16),
        buf(6, 2, 3, COLS, LO, dtype=BF16),
        buf(2, 3, WIDE, LO, dtype=BF16), buf(1, 3, WIDE, LO, dtype=BF16), buf(2, 3, WIDE, LO, dtype=BF16),
        buf(8, 2, 3, WIDE, LO, dtype=BF16),
        buf(3, 1, 3, WIDE, LO, dtype=BF16), buf(3, 2, 3, WIDE, LO, dtype=BF16),
        buf(4, 1, 3, WIDE, LO, dtype=BF16), buf(4, 2, 3, WIDE, LO, dtype=BF16),
        buf(3, CELLS, LO), buf(CELLS, LO), buf(6, 49, 8, LO),
        buf(256, HID, dtype=BF16), buf(256, HID, dtype=BF16),
        buf(256, HID), buf(CH, HID), buf(2, 49, 8, LO), buf(2 * HALF, LO),
        buf(HALF, LO, dtype=BF16), buf(HALF, LO, dtype=BF16),
        buf(16, PIECE, LO, dtype=BF16), buf(15, PIECE, LO, dtype=BF16), buf(4, PIECE, LO),
        buf(2, 16, PIECE, LO, dtype=BF16),
        pltpu.SemaphoreType.DMA((COPIES,)), pltpu.SemaphoreType.DMA((COPIES,)),
    ]
    outs = (
        jax.ShapeDtypeStruct((ROWS, COLS, CH), BF16),
        jax.ShapeDtypeStruct((ROWS, COLS, CH), F32),
        jax.ShapeDtypeStruct((7, 7, CH), F32),
        jax.ShapeDtypeStruct((CH, HID), F32),
        jax.ShapeDtypeStruct((CH, HID), F32),
    )
    found = pl.pallas_call(
        kernel,
        out_shape=outs,
        in_specs=[anywhere] * 13,
        out_specs=(vmem,) * 5,
        scratch_shapes=scratch,
        compiler_params=pltpu.CompilerParams(
            collective_id=0, has_side_effects=True, vmem_limit_bytes=60 * 1024 * 1024
        ),
        name="block",
    )(
        states, grad_out, land_mask, partner, dw_kernel, row(dw_bias), row(ln_gain), row(ln_bias),
        w_in, b_in.reshape(HID // LO, LO), w_out.T, row(b_out), row(layer_scale),
    )
    out_a, grad_states, grad_kernel, grad_win, grad_wout = pl.pallas_call(
        move,
        out_shape=outs,
        in_specs=[anywhere] * 5,
        out_specs=(anywhere,) * 5,
        scratch_shapes=[pltpu.VMEM(o.shape, o.dtype) for o in outs]
        + [pltpu.SemaphoreType.DMA((5,)), pltpu.SemaphoreType.DMA((5,))],
        name="move",
    )(*found)
    return out_a, grad_states, grad_kernel, grad_win, grad_wout.T


def solution(mesh):
    placed = (
        P(None, "lat", "lon", None), P("lat", "lon", None), P("lat", "lon"),
        P(), P(), P(), P(), P(), P(), P(), P(), P(), P(),
    )
    return jax.shard_map(
        shards,
        mesh=mesh,
        in_specs=placed,
        out_specs=(P("lat", "lon", None), P("lat", "lon", None), P(), P(), P()),
        check_vma=False,
    )
```

```python
import functools
import math

import jax
import jax.numpy as jnp
from jax import lax
from jax.experimental import pallas as pl
from jax.experimental.pallas import tpu as pltpu
from jax.sharding import PartitionSpec as P

F32 = jnp.float32
BF16 = jnp.bfloat16
MESH = pl.DeviceIdType.MESH

ROWS = 16
COLS = 64
PROWS = 22
WIDE = 80
LO = 128
CH = 192
HID = 768
NLON = 2048
CELLS = ROWS * COLS
CHUNK = 256
PIECE = 80
HALF = 16 * PIECE
QUART = 4 * PIECE
WIN_AT, WOUT_AT, REST_AT = 0, 1152, 2304

root_factor = math.sqrt(2.0 / math.pi)
cubic_coef = 0.044715
norm_eps = 1e-06
scale = 1.0 / math.sqrt(64 * NLON)

LAT_AT, LON_AT, FIELD = 0, 2, 8
FOLD_B, FOLD_A, FOLD_Z, ROUND = 16, 30, 44, 6
S0_AT, S1_AT, S3_AT, G1_AT, G3_AT = 58, 59, 74, 77, 92
K0_AT, K1_AT, K3_AT, K4_AT = 96, 97, 112, 115
COPIES = 130


def dot(a, b, dims=((1,), (0,))):
    return lax.dot_general(a, b, (dims, ((), ())), preferred_element_type=F32)


def kernel(
    x_in, go_in, mask_in, partner_in, dw_in, dwb_in, g_in, lb_in, win_in, bin_in,
    wout_in, bout_in, ls_in,
    outa_out, gs_out, gk_ref, ag_out,
    x_ref, go_ref, mask_ref, partner_ref, dw_ref, dwb_ref, g_ref, lb_ref, win_ref, bin_ref,
    wout_ref, bout_ref, ls_ref, load_sem, outa_ref, gs_ref, store_sem, gkf, kr0, ksum, kr1, kr3, kag,
    pd, pz, xb, zb, sx, sz, rlx, rlz, rcx, rcz, fb1, fa1, fz1, vb, va, vz, fb2, fya, fyz, fxa, fxz,
    dp, mb, kt, wa, wb, gw, gwo, gka, flat, b0, r0, hb, r1, r3, ag, ssem, rsem,
):
    lon = lax.axis_index("lon")
    lat = lax.axis_index("lat")
    top = lat == 3
    xx, yh, zz = lon // 8, (lon // 4) % 2, lon % 4
    yl, core = lat // 2, lat % 2
    yy = yh * 2 + yl

    def lon_of(step):
        return (lon + step + 64) % 32

    mate = (lon, lat + 1 - 2 * core)

    def plane_peer(m):
        return (((xx + m // 4) % 4) * 8 + yh * 4 + (zz + m % 4) % 4, lat)

    def third_peer(k):
        far = (yy + k) % 4
        return (xx * 8 + (far // 2) * 4 + zz, (far % 2) * 2 + core)

    place = xx * 4 + zz

    def place_of(m):
        return ((xx + m // 4) % 4) * 4 + (zz + m % 4) % 4

    block8 = lon // 4
    mirror = lon + 3 - 2 * zz
    own1 = 2 * zz - 3
    own2 = (2 * block8 + 1) % 8

    def mirror_of(v):
        return v + 3 - 2 * (v % 4)

    def fold1_to(k):
        return mirror_of(lon_of(-k))

    def fold1_from(k):
        return (mirror + k) % 32

    def fold2_peer(k):
        return ((7 - block8 + k) % 8) * 4 + zz

    def remote(src, dst, i, peer):
        return pltpu.make_async_remote_copy(
            src_ref=src, dst_ref=dst, send_sem=ssem.at[i], recv_sem=rsem.at[i],
            device_id={"lon": peer[0], "lat": peer[1]}, device_id_type=MESH,
        )

    barrier = pltpu.get_barrier_semaphore()

    def greet(peer):
        pl.semaphore_signal(
            barrier, inc=1, device_id={"lon": peer[0], "lat": peer[1]}, device_id_type=MESH
        )

    greet(mate)
    for m in range(1, 16):
        greet(plane_peer(m))
    for k in (1, 2, 3):
        greet(third_peer(k))
    for side in (-1, 1):
        greet((lon_of(side), lat))
    for dl in (-1, 1):
        @pl.when((lat + dl >= 0) & (lat + dl <= 3))
        def _():
            for side in (-1, 0, 1):
                greet((lon_of(side), lat + dl))

    @pl.when(top)
    def _():
        for k in range(6):
            @pl.when(k != own1)
            def _(k=k):
                greet((fold1_from(k), lat))
        for k in range(8):
            @pl.when(k != own2)
            def _(k=k):
                greet((fold2_peer(k), lat))

    ins = (x_in, go_in, mask_in, partner_in, dw_in, dwb_in, g_in, lb_in, win_in, bin_in,
           wout_in, bout_in, ls_in)
    held = (x_ref, go_ref, mask_ref, partner_ref, dw_ref, dwb_ref, g_ref, lb_ref, win_ref, bin_ref,
            wout_ref, bout_ref, ls_ref)
    loads = [pltpu.make_async_copy(a, b, load_sem.at[i]) for i, (a, b) in enumerate(zip(ins, held))]
    for load in loads:
        load.start()
    loads[0].wait()

    def at(plane, row, col):
        return (plane * PROWS + row) * WIDE + col

    def spread(r, carry):
        a = x_ref[0, r].astype(F32)
        b = x_ref[1, r].astype(F32)
        mix = jnp.concatenate([a[:, LO:], b[:, LO:]], axis=1)
        for plane, v in enumerate((a[:, :LO], b[:, :LO], mix)):
            pd[pl.ds(pl.multiple_of(at(plane, 3 + r, 8), 8), COLS), :] = v
            xb[plane, r] = v.astype(BF16)
        return carry

    lax.fori_loop(0, ROWS, spread, 0)

    def pack(field, send, planes):
        for plane in range(planes):
            for k in range(3):
                send[0, plane, k] = field[pl.ds(at(plane, 3, 8 + k), ROWS, stride=WIDE), :].astype(BF16)
                send[1, plane, k] = field[pl.ds(at(plane, 3, 69 + k), ROWS, stride=WIDE), :].astype(BF16)

    pack(pd, sx, 3)

    peers = 21 + jnp.where(lat > 0, 3, 0) + jnp.where(lat < 3, 3, 0)
    peers = peers + jnp.where(top, 13 - jnp.where(zz >= 2, 1, 0), 0)
    pl.semaphore_wait(barrier, peers)

    def lat_copies(base, block, got):
        return (
            (lat < 3, remote(block.at[:, 13:16], got.at[0], base + LAT_AT, (lon, lat + 1))),
            (lat > 0, remote(block.at[:, 0:3], got.at[1], base + LAT_AT + 1, (lon, lat - 1))),
        )

    def lon_copies(base, send, got):
        found = []
        for side in range(2):
            for slot in range(3):
                dl = 1 - slot
                found.append((
                    (lat + dl >= 0) & (lat + dl <= 3),
                    remote(
                        send.at[1 - side], got.at[side, slot], base + LON_AT + 3 * side + slot,
                        (lon_of(1 - 2 * side), lat + dl),
                    ),
                ))
        return found

    def lon_arrives(slot):
        return (lat + slot - 1 >= 0) & (lat + slot - 1 <= 3)

    def fold1_copies(base, block, planes, got):
        found = []
        for k in range(6):
            width = 16 if k == 5 else COLS
            found.append((k != own1, remote(
                block.at[planes, 13:16, 0:width], got.at[k, :, :, 0:width], base + k,
                (fold1_to(k), lat),
            )))
        return found

    def fold2_copies(base, window, got):
        return [
            (k != own2, remote(window, got.at[k], base + ROUND + k, (fold2_peer(k), lat)))
            for k in range(8)
        ]

    def start_fold(base, block, planes, f1):
        for cond, copy in fold1_copies(base, block, planes, f1):
            pl.when(cond)(copy.start)

    def start_halo(base, block, send, rl, rc):
        for cond, copy in lon_copies(base, send, rc):
            pl.when(cond)(copy.start)
        for cond, copy in lat_copies(base, block, rl):
            pl.when(cond)(copy.start)

    def finish_halo(base, field, planes, block, send, rl, rc):
        lats = lat_copies(base, block, rl)
        for way, (arrives, row) in enumerate(((lat > 0, 0), (lat < 3, 19))):
            @pl.when(arrives)
            def _(way=way, row=row):
                lats[way][1].wait_recv()
                for plane in range(planes):
                    for r in range(3):
                        field[pl.ds(at(plane, row + r, 8), COLS), :] = rl[way, plane, r].astype(F32)
        lons = lon_copies(base, send, rc)
        for side in range(2):
            col = 5 if side == 0 else 72
            for slot in range(3):
                @pl.when(lon_arrives(slot))
                def _(side=side, slot=slot, col=col):
                    lons[3 * side + slot][1].wait_recv()
                    for plane in range(planes):
                        for k in range(3):
                            v = rc[side, slot, plane, k].astype(F32)
                            if slot == 1:
                                field[pl.ds(at(plane, 3, col + k), ROWS, stride=WIDE), :] = v
                            else:
                                for r in range(3):
                                    row = r if slot == 0 else 19 + r
                                    own = 13 + r if slot == 0 else r
                                    field[pl.ds(at(plane, row, col + k), 1), :] = v[own:own + 1]

    def shift_parts():
        begin = lax.rem(partner_ref[0] + (NLON - 2), NLON)
        return lax.rem(begin, COLS), lax.rem(lax.div(begin, COLS), 4), lax.div(begin, 4 * COLS)

    def make_window(base, block, planes, f1, window):
        offset, near, _ = shift_parts()
        for cond, copy in fold1_copies(base, block, planes, f1):
            pl.when(cond)(copy.wait_recv)

        @pl.when(zz >= 2)
        def _():
            f1[own1] = block[planes, 13:16]

        slot_at = lax.broadcasted_iota(jnp.int32, (WIDE, 3 * COLS), 0)
        from_at = lax.broadcasted_iota(jnp.int32, (WIDE, 3 * COLS), 1)
        pick = jnp.where(from_at + slot_at == offset + 74, 1.0, 0.0).astype(BF16)
        for plane in range(window.shape[0]):
            for r in range(3):
                three = jnp.concatenate([f1[near + c, plane, r] for c in range(3)], axis=0)
                window[plane, r] = dot(pick, three).astype(BF16)

    def middle_fold(base, block, planes, f1, window, f2):
        make_window(base, block, planes, f1, window)
        for cond, copy in fold2_copies(base, window, f2):
            pl.when(cond)(copy.start)
        f2[own2] = window[...]

    def foldy_copy(base, window, fy):
        return remote(window, fy.at[yh], base + ROUND, (xx * 8 + (1 - yh) * 4 + zz, lat))

    def foldy_from(base, window, fy):
        return remote(window, fy.at[1 - yh], base + ROUND, (xx * 8 + (1 - yh) * 4 + zz, lat))

    def foldx_copies(base, fy, fx):
        return [
            remote(fy.at[2], fx.at[xx], base + ROUND + k, (((xx + k) % 4) * 8 + yh * 4 + zz, lat))
            for k in (1, 2, 3)
        ]

    def foldx_from(base, fy, fx):
        return [
            remote(fy.at[2], fx.at[(xx + 4 - k) % 4], base + ROUND + k, (((xx + k) % 4) * 8 + yh * 4 + zz, lat))
            for k in (1, 2, 3)
        ]

    def fold_to_y(base, block, planes, f1, window, fy):
        make_window(base, block, planes, f1, window)
        foldy_copy(base, window, fy).start()
        fy[yh] = window[...]

    def fold_to_x(base, window, fy, fx):
        foldy_from(base, window, fy).wait_recv()
        far = shift_parts()[2]
        chosen = fy[lax.rem(1 - yh + far, 2)]
        fy[2] = chosen
        for copy in foldx_copies(base, fy, fx):
            copy.start()
        fx[xx] = chosen

    def end_fold(base, field, first, fy, fx):
        for copy in foldx_from(base, fy, fx):
            copy.wait_recv()
        far = shift_parts()[2]
        source = lax.div(lax.rem(7 - block8 + far, 8), 2)
        for plane in range(fx.shape[1]):
            for k in range(3):
                field[pl.ds(at(first + plane, 19 + k, 0), WIDE), :] = fx[source, plane, 2 - k].astype(F32)

    def close_three(base, block, planes, f1, window, fy, fx):
        for cond, copy in fold1_copies(base, block, planes, f1):
            pl.when(cond)(copy.wait_send)
        foldy_copy(base, window, fy).wait_send()
        for copy in foldx_copies(base, fy, fx):
            copy.wait_send()

    def finish_fold(base, field, first, window, f2):
        for cond, copy in fold2_copies(base, window, f2):
            pl.when(cond)(copy.wait_recv)
        far = shift_parts()[2]
        for plane in range(window.shape[0]):
            for k in range(3):
                field[pl.ds(at(first + plane, 19 + k, 0), WIDE), :] = f2[far, plane, 2 - k].astype(F32)

    def close_fold(base, block, planes, f1, window, f2):
        for cond, copy in fold1_copies(base, block, planes, f1):
            pl.when(cond)(copy.wait_send)
        for cond, copy in fold2_copies(base, window, f2):
            pl.when(cond)(copy.wait_send)

    def close_field(base, block, send, rl, rc):
        for cond, copy in lat_copies(base, block, rl):
            pl.when(cond)(copy.wait_send)
        for cond, copy in lon_copies(base, send, rc):
            pl.when(cond)(copy.wait_send)

    in_b, in_a, in_z = slice(1, 3), slice(0, 1), slice(0, 2)

    @pl.when(top)
    def _():
        start_fold(FOLD_B, xb, in_b, fb1)

    start_halo(0, xb, sx, rlx, rcx)

    for load in loads[1:]:
        load.wait()

    def clear_south(field, planes):
        for plane in range(planes):
            field[pl.ds(at(plane, 0, 0), 3 * WIDE), :] = jnp.zeros((3 * WIDE, LO), F32)

    clear_south(pd, 3)
    clear_south(pz, 2)

    lane = lax.broadcasted_iota(jnp.int32, (1, LO), 1)
    upper = lane >= 64

    def table(a, carry):
        low, high = dw_ref[a][:, :LO], dw_ref[a][:, LO:]
        mix = jnp.concatenate([high, high], axis=1)
        rlow, rhigh = dw_ref[6 - a][:, :LO], dw_ref[6 - a][:, LO:]
        rmix = jnp.concatenate([rhigh, rhigh], axis=1)
        for b in range(7):
            for kind, (v, w) in enumerate(((low, rlow), (mix, rmix))):
                straight = jnp.broadcast_to(v[b:b + 1], (8, LO))
                turned = jnp.broadcast_to(w[6 - b:7 - b], (8, LO))
                kt[kind, a * 7 + b] = straight
                kt[2 + kind, a * 7 + b] = turned
                kt[4 + kind, a * 7 + b] = jnp.where(top, straight, turned)
        return carry

    lax.fori_loop(0, 7, table, 0)
    wa[0:192] = win_ref[...]
    wa[192:256] = jnp.zeros((64, HID), BF16)
    wb[0:128] = win_ref[0:128]
    wb[128:192] = jnp.zeros((64, HID), BF16)
    wb[192:256] = win_ref[128:192]
    eye = jnp.where(
        lax.broadcasted_iota(jnp.int32, (COLS, COLS), 0) == lax.broadcasted_iota(jnp.int32, (COLS, COLS), 1),
        1.0, 0.0,
    ).astype(BF16)
    mask_t = dot(eye, mask_ref[...].astype(F32).astype(BF16), ((1,), (1,))).astype(BF16)
    for r in range(ROWS):
        one = jnp.where(lax.broadcasted_iota(jnp.int32, (ROWS, LO), 0) == r, 1.0, 0.0).astype(BF16)
        mb[r * COLS:(r + 1) * COLS] = dot(mask_t, one)
    gw[...] = jnp.zeros_like(gw)
    gwo[...] = jnp.zeros_like(gwo)
    gka[...] = jnp.zeros_like(gka)
    flat[REST_AT:2560] = jnp.zeros((2560 - REST_AT, LO), F32)
    gkf[112:128] = jnp.zeros((16, LO), F32)
    for f1 in (fb1, fa1, fz1):
        f1[5, :, :, 16:64] = jnp.zeros_like(f1[5, :, :, 16:64])


    zero64 = jnp.zeros((1, 64), F32)

    def halves(ref, state):
        v = ref[...]
        high = v[:, LO:]
        parts = [high, zero64] if state == 0 else [zero64, high]
        return v[:, :LO], jnp.concatenate(parts, axis=1)

    def conv(field, plane, c, half, tab, tab_last):
        base = at(plane, 4 * c, 32 * half + 5)
        acc = [[jnp.zeros((8, LO), F32) for _ in range(4)] for _ in range(4)]
        for p in range(10):
            for b in range(7):
                use = tab_last if p >= 7 else tab
                ks = {r: kt[use, (p - r) * 7 + b] for r in range(4) if 0 <= p - r <= 6}
                for t in range(4):
                    v = field[pl.ds(base + p * WIDE + 8 * t + b, 8), :]
                    for r, kv in ks.items():
                        acc[r][t] = acc[r][t] + kv * v
        return acc

    def bias(s):
        return jnp.concatenate([bin_ref[2 * s:2 * s + 1], bin_ref[2 * s + 1:2 * s + 2]], axis=1)

    def norm(c, state):
        here = pl.ds(pl.multiple_of(c * CHUNK, CHUNK), CHUNK)
        keep = upper if state == 1 else jnp.logical_not(upper)
        blo, bhi = halves(dwb_ref, state)
        glo, ghi = halves(g_ref, state)
        llo, lhi = halves(lb_ref, state)
        lo = dp[state, here] + blo
        hi = jnp.where(keep, dp[2, here] + bhi, 0.0)
        mean = jnp.sum(lo + hi, axis=1, keepdims=True) * (1.0 / CH)
        lo = lo - mean
        hi = jnp.where(keep, hi - mean, 0.0)
        inv = lax.rsqrt(jnp.sum(lo * lo + hi * hi, axis=1, keepdims=True) * (1.0 / CH) + norm_eps)
        nlo, nhi = lo * inv, hi * inv
        low = jnp.concatenate(
            [(nlo * glo + llo).astype(BF16), (nhi * ghi + lhi).astype(BF16)], axis=1
        )
        return low, nlo, nhi, inv, glo, ghi, keep

    def forward_chunk(c):
        low = norm(c, 0)[0]
        mixed = jnp.broadcast_to(bout_ref[...], (CHUNK, CH))
        for s in range(3):
            cut = slice(256 * s, 256 * s + 256)
            u = dot(low, wa[:, cut]) + bias(s)
            t = jnp.tanh(u * (root_factor + (root_factor * cubic_coef) * (u * u)))
            act = (u * (0.5 + 0.5 * t)).astype(BF16)
            mixed = mixed + dot(act, wout_ref[:, cut], ((1,), (1,)))
        mixed = mixed * ls_ref[...]
        here = pl.ds(pl.multiple_of(c * CHUNK, CHUNK), CHUNK)
        m = mb[here]
        mm = jnp.concatenate([m, m[:, :64]], axis=1)
        for r in range(4):
            cut = slice(64 * r, 64 * r + 64)
            outa_ref[4 * c + r] = (x_ref[0, 4 * c + r].astype(F32) + mm[cut] * mixed[cut]).astype(BF16)

    def backward_chunk(c):
        low, nlo, nhi, inv, glo, ghi, keep = norm(c, 1)
        here = pl.ds(pl.multiple_of(c * CHUNK, CHUNK), CHUNK)
        m = mb[here]
        mm = jnp.concatenate([m, m[:, :64]], axis=1)
        go = jnp.concatenate([go_ref[4 * c + r] for r in range(4)], axis=0).astype(F32)
        gl = (mm * (ls_ref[...] * go)).astype(BF16)
        gn = jnp.zeros((CHUNK, 256), F32)
        for s in range(3):
            cut = slice(256 * s, 256 * s + 256)
            u = dot(low, wb[:, cut]) + bias(s)
            u2 = u * u
            t = jnp.tanh(u * (root_factor + (root_factor * cubic_coef) * u2))
            half = 0.5 + 0.5 * t
            value = u * half
            slope = half + value * (1.0 - t) * (root_factor + (3.0 * root_factor * cubic_coef) * u2)
            act = value.astype(BF16)
            gwo[:, cut] += dot(gl, act, ((0,), (0,)))
            gh = (dot(gl, wout_ref[:, cut]) * slope).astype(BF16)
            gw[:, cut] += dot(low, gh, ((0,), (0,)))
            gn = gn + dot(gh, wb[:, cut], ((1,), (1,)))
        nl, nh = gn[:, :LO] * glo, gn[:, LO:] * ghi
        one = jnp.sum(nl + nh, axis=1, keepdims=True) * (1.0 / CH)
        two = jnp.sum(nl * nlo + nh * nhi, axis=1, keepdims=True) * (1.0 / CH)
        zl = inv * (nl - one - nlo * two)
        zh = jnp.where(keep, inv * (nh - one - nhi * two), 0.0)
        for plane, v in enumerate((zl, zh)):
            for r in range(4):
                cut = slice(64 * r, 64 * r + 64)
                pz[pl.ds(pl.multiple_of(at(plane, 3 + 4 * c + r, 8), 8), COLS), :] = v[cut]
                zb[plane, 4 * c + r] = v[cut].astype(BF16)

    def sweep_states(plane, c):
        def sweep(half, carry):
            kind = plane // 2
            acc = conv(pd, plane, c, half, kind, kind)
            for r in range(4):
                for t in range(4):
                    cell = pl.multiple_of(c * CHUNK + r * COLS + half * 32 + 8 * t, 8)
                    dp[plane, pl.ds(cell, 8)] = acc[r][t]
            return carry

        lax.fori_loop(0, 2, sweep, 0)

    def kernel_chunk(c):
        for plane in range(2):
            for rows in ((0, 1, 2, 3), (4, 5, 6)):
                def add_row(i, acc, plane=plane, rows=rows):
                    acc = list(acc)
                    for t in range(8):
                        z = pz[pl.ds(pl.multiple_of(at(plane, 3 + i, 8 + 8 * t), 8), 8), :]
                        for n, a in enumerate(rows):
                            for b in range(7):
                                v = pd[pl.ds(at(1 + plane, i + a, 5 + 8 * t + b), 8), :]
                                acc[n * 7 + b] = acc[n * 7 + b] + v * z
                    return tuple(acc)

                acc = lax.fori_loop(
                    4 * c, 4 * c + 4, add_row,
                    tuple(jnp.zeros((8, LO), F32) for _ in range(7 * len(rows))),
                )
                for n, a in enumerate(rows):
                    for b in range(7):
                        gka[plane, a * 7 + b] += acc[n * 7 + b]

    @pl.when(top)
    def _():
        middle_fold(FOLD_B, xb, in_b, fb1, vb, fb2)
        start_fold(FOLD_A, xb, in_a, fa1)

    finish_halo(0, pd, 3, xb, sx, rlx, rcx)

    def first_pass(c, carry):
        @pl.when(top & (c == 3))
        def _():
            finish_fold(FOLD_B, pd, 1, vb, fb2)
            fold_to_y(FOLD_A, xb, in_a, fa1, va, fya)

        def both(plane, carry):
            sweep_states(plane, c)
            return carry

        lax.fori_loop(1, 3, both, 0)

        backward_chunk(c)
        return carry

    lax.fori_loop(0, 4, first_pass, 0)

    for s in range(6):
        cut = slice(128 * s, 128 * s + 128)
        flat[WIN_AT + 192 * s:WIN_AT + 192 * s + 128] = gw[0:128, cut]
        flat[WIN_AT + 192 * s + 128:WIN_AT + 192 * s + 192] = gw[192:256, cut]
        flat[WOUT_AT + 192 * s:WOUT_AT + 192 * s + 192] = gwo[:, cut]

    def half_at(which):
        return pl.ds(pl.multiple_of(which * HALF, 8), HALF)

    b0[...] = flat[half_at(1 - core)].astype(BF16)
    s0 = remote(b0, r0, S0_AT, mate)

    def s1(m):
        return remote(hb.at[place_of(m)], r1.at[m - 1], S1_AT + m - 1, plane_peer(m))

    def s3(k):
        return remote(r3.at[yy], r3.at[yy], S3_AT + k - 1, third_peer(k))

    def s3_from(k):
        return remote(r3.at[yy], r3.at[(yy + 4 - k) % 4], S3_AT + k - 1, third_peer(k))

    def g1(m):
        return remote(ag.at[core, place], ag.at[core, place], G1_AT + m - 1, plane_peer(m))

    def g1_from(m):
        there = ((xx + 4 - m // 4) % 4) * 4 + (zz + 4 - m % 4) % 4
        return remote(ag.at[core, place], ag.at[core, there], G1_AT + m - 1, plane_peer(m))

    def g3(d):
        rows = pl.ds(pl.multiple_of(((xx + 4 - d) % 4) * 4, 4), 4)
        return remote(ag.at[core, rows], ag.at[core, rows], G3_AT + d, mate)

    def g3_from(d):
        rows = pl.ds(pl.multiple_of(((xx + 4 - d) % 4) * 4, 4), 4)
        return remote(ag.at[core, rows], ag.at[1 - core, rows], G3_AT + d, mate)

    k0 = remote(gkf, kr0, K0_AT, mate)

    def k1(m):
        return remote(ksum.at[place_of(m)], kr1.at[m - 1], K1_AT + m - 1, plane_peer(m))

    def k3(k):
        return remote(kr3.at[yy], kr3.at[yy], K3_AT + k - 1, third_peer(k))

    def k3_from(k):
        return remote(kr3.at[yy], kr3.at[(yy + 4 - k) % 4], K3_AT + k - 1, third_peer(k))

    def k4(m):
        return remote(kag.at[place], kag.at[place], K4_AT + m - 1, plane_peer(m))

    def k4_from(m):
        there = ((xx + 4 - m // 4) % 4) * 4 + (zz + 4 - m % 4) % 4
        return remote(kag.at[place], kag.at[there], K4_AT + m - 1, plane_peer(m))

    s0.start()

    pack(pz, sz, 2)

    @pl.when(top)
    def _():
        start_fold(FOLD_Z, zb, in_z, fz1)

    start_halo(FIELD, zb, sz, rlz, rcz)

    def second_pass(c, carry):
        @pl.when(c == 2)
        def _():
            s0.wait_recv()
            for i in range(16):
                part = pl.ds(pl.multiple_of(core * HALF + i * PIECE, 8), PIECE)
                total = flat[part] + r0[i * PIECE:(i + 1) * PIECE].astype(F32)
                flat[part] = total
                hb[i] = total.astype(BF16)
            for m in range(1, 16):
                s1(m).start()

        @pl.when(top & (c == 2))
        def _():
            fold_to_x(FOLD_A, va, fya, fxa)

        kernel_chunk(c)
        return carry

    lax.fori_loop(0, 4, second_pass, 0)

    for plane in range(2):
        for n in range(49):
            line = plane * 56 + n
            gkf[line:line + 1] = jnp.sum(gka[plane, n], axis=0, keepdims=True)
        gkf[plane * 56 + 49:plane * 56 + 56] = jnp.zeros((7, LO), F32)
    k0.start()

    def state_pass(c, carry):
        @pl.when(c == 2)
        def _():
            k0.wait_recv()
            for i in range(16):
                ksum[i] = gkf[8 * i:8 * i + 8] + kr0[8 * i:8 * i + 8]
            for m in range(1, 16):
                k1(m).start()

        sweep_states(0, c)
        forward_chunk(c)
        return carry

    lax.fori_loop(0, 3, state_pass, 0)

    finish_halo(FIELD, pz, 2, zb, sz, rlz, rcz)

    @pl.when(top)
    def _():
        fold_to_y(FOLD_Z, zb, in_z, fz1, vz, fyz)

    stores = [
        pltpu.make_async_copy(outa_ref, outa_out, store_sem.at[0]),
        pltpu.make_async_copy(gs_ref, gs_out, store_sem.at[1]),
        pltpu.make_async_copy(ag.at[core], ag_out.at[core], store_sem.at[2]),
        pltpu.make_async_copy(ag.at[1 - core], ag_out.at[1 - core], store_sem.at[3]),
    ]

    def third_pass(c, carry):
        @pl.when(c == 1)
        def _():
            for m in range(1, 16):
                s1(m).wait_recv()
            total = flat[pl.ds(pl.multiple_of(core * HALF + place * PIECE, 8), PIECE)]
            for m in range(15):
                total = total + r1[m].astype(F32)
            r3[yy] = total
            for k in (1, 2, 3):
                s3(k).start()

        @pl.when(c == 2)
        def _():
            for m in range(1, 16):
                k1(m).wait_recv()
            total = ksum[place]
            for m in range(15):
                total = total + kr1[m]
            kr3[yy] = total
            for k in (1, 2, 3):
                k3(k).start()

        @pl.when(top & (c == 2))
        def _():
            fold_to_x(FOLD_Z, vz, fyz, fxz)

        @pl.when(c == 3)
        def _():
            for k in (1, 2, 3):
                s3_from(k).wait_recv()
            ag[core, place] = ((r3[0] + r3[1] + r3[2] + r3[3]) * scale).astype(BF16)
            for m in range(1, 16):
                g1(m).start()

        @pl.when(top & (c == 3))
        def _():
            end_fold(FOLD_A, pd, 0, fya, fxa)

        @pl.when(c == 3)
        def _():
            sweep_states(0, 3)
            forward_chunk(3)
            stores[0].start()
            for k in (1, 2, 3):
                k3_from(k).wait_recv()
            kag[place] = (kr3[0] + kr3[1] + kr3[2] + kr3[3]) * scale
            for m in range(1, 16):
                k4(m).start()

        @pl.when(top & (c == 3))
        def _():
            end_fold(FOLD_Z, pz, 0, fyz, fxz)

        last = jnp.where(c == 3, 4, 2)

        def sweep(half, carry):
            at_col = pl.ds(pl.multiple_of(32 * half, 32), 32)
            acc_lo = conv(pz, 0, c, half, 2, last)
            for r in range(4):
                low = jnp.concatenate(acc_lo[r], axis=0)
                go = go_ref[4 * c + r, at_col, :].astype(F32)
                gs_ref[4 * c + r, at_col, 0:LO] = low + go[:, :LO]
            acc_hi = conv(pz, 1, c, half, 3, last + 1)
            for r in range(4):
                high = jnp.concatenate(acc_hi[r], axis=0)
                go = go_ref[4 * c + r, at_col, :].astype(F32)
                gs_ref[4 * c + r, at_col, LO:CH] = high[:, 64:] + go[:, LO:]
            return carry

        lax.fori_loop(0, 2, sweep, 0)
        return carry

    lax.fori_loop(0, 4, third_pass, 0)

    stores[1].start()
    for d in (0, 1, 3, 2):
        for m in range(max(4 * d, 1), 4 * d + 4):
            g1_from(m).wait_recv()
        g3(d).start()
    stores[2].start()
    for m in range(1, 16):
        k4_from(m).wait_recv()
    kall = jnp.concatenate([kag[i] for i in range(14)], axis=0)
    for a in range(7):
        gk_ref[a, :, 0:LO] = kall[7 * a:7 * a + 7]
        gk_ref[a, :, LO:CH] = kall[56 + 7 * a:56 + 7 * a + 7, 64:]
    for d in range(4):
        g3_from(d).wait_recv()
    stores[3].start()

    close_field(0, xb, sx, rlx, rcx)
    close_field(FIELD, zb, sz, rlz, rcz)

    @pl.when(top)
    def _():
        close_fold(FOLD_B, xb, in_b, fb1, vb, fb2)
        close_three(FOLD_A, xb, in_a, fa1, va, fya, fxa)
        close_three(FOLD_Z, zb, in_z, fz1, vz, fyz, fxz)

    s0.wait_send()
    for m in range(1, 16):
        s1(m).wait_send()
        g1(m).wait_send()
    for k in (1, 2, 3):
        s3(k).wait_send()
    for d in range(4):
        g3(d).wait_send()
    k0.wait_send()
    for m in range(1, 16):
        k1(m).wait_send()
        k4(m).wait_send()
    for k in (1, 2, 3):
        k3(k).wait_send()
    for store in stores:
        store.wait()


def part_of(ag, start, size):
    first, end = start // PIECE, -(-(start + size) // PIECE)
    found = [ag[i // 16, i % 16] for i in range(first, end)]
    return jnp.concatenate(found, axis=0)[start - first * PIECE:start - first * PIECE + size].astype(F32)


def finish(
    outa_in, gs_in, gk_in, ag_in, outa_out, gs_out, gk_out, gwin_out, gwout_out,
    outa, gs, gk, ag, gwin, gwout, come, go,
):
    first = [
        pltpu.make_async_copy(a, b, come.at[i])
        for i, (a, b) in enumerate(((ag_in, ag), (gs_in, gs), (outa_in, outa), (gk_in, gk)))
    ]
    second = [
        pltpu.make_async_copy(a, b, go.at[i])
        for i, (a, b) in enumerate(((gs, gs_out), (outa, outa_out), (gk, gk_out), (gwin, gwin_out), (gwout, gwout_out)))
    ]
    for copy in first:
        copy.start()
    first[0].wait()
    for s in range(6):
        gwin[:, 128 * s:128 * s + 128] = part_of(ag, WIN_AT + 192 * s, 192)
    second[3].start()
    for i in range(3):
        first[i + 1].wait()
        second[i].start()
    for s in range(6):
        gwout[:, 128 * s:128 * s + 128] = part_of(ag, WOUT_AT + 192 * s, 192)
    second[4].start()
    for copy in second:
        copy.wait()


def shards(states, grad_out, land_mask, partner, dw_kernel, dw_bias, ln_gain, ln_bias, w_in, b_in,
           w_out, b_out, layer_scale):
    def row(v):
        return v.reshape(1, v.shape[0])

    vmem = pl.BlockSpec(memory_space=pltpu.VMEM)
    anywhere = pl.BlockSpec(memory_space=pl.ANY)

    def buf(*shape, dtype=F32):
        return pltpu.VMEM(shape, dtype)

    load_to = [
        buf(2, ROWS, COLS, CH, dtype=BF16), buf(ROWS, COLS, CH, dtype=BF16),
        buf(ROWS, COLS, dtype=jnp.int32), pltpu.SMEM((NLON,), jnp.int32), buf(7, 7, CH),
        buf(1, CH), buf(1, CH), buf(1, CH), buf(CH, HID, dtype=BF16), buf(HID // LO, LO),
        buf(CH, HID, dtype=BF16), buf(1, CH), buf(1, CH), pltpu.SemaphoreType.DMA((13,)),
        buf(ROWS, COLS, CH, dtype=BF16), buf(ROWS, COLS, CH), pltpu.SemaphoreType.DMA((4,)),
        buf(128, LO), buf(128, LO), buf(16, 8, LO), buf(15, 8, LO), buf(4, 8, LO), buf(16, 8, LO),
    ]
    scratch = load_to + [
        buf(3 * PROWS * WIDE, LO), buf(2 * PROWS * WIDE, LO),
        buf(3, ROWS, COLS, LO, dtype=BF16), buf(2, ROWS, COLS, LO, dtype=BF16),
        buf(2, 3, 3, ROWS, LO, dtype=BF16), buf(2, 2, 3, ROWS, LO, dtype=BF16),
        buf(2, 3, 3, COLS, LO, dtype=BF16), buf(2, 2, 3, COLS, LO, dtype=BF16),
        buf(2, 3, 3, 3, ROWS, LO, dtype=BF16), buf(2, 3, 2, 3, ROWS, LO, dtype=BF16),
        buf(6, 2, 3, COLS, LO, dtype=BF16), buf(6, 1, 3, COLS, LO, dtype=BF16),
        buf(6, 2, 3, COLS, LO, dtype=BF16),
        buf(2, 3, WIDE, LO, dtype=BF16), buf(1, 3, WIDE, LO, dtype=BF16), buf(2, 3, WIDE, LO, dtype=BF16),
        buf(8, 2, 3, WIDE, LO, dtype=BF16),
        buf(3, 1, 3, WIDE, LO, dtype=BF16), buf(3, 2, 3, WIDE, LO, dtype=BF16),
        buf(4, 1, 3, WIDE, LO, dtype=BF16), buf(4, 2, 3, WIDE, LO, dtype=BF16),
        buf(3, CELLS, LO), buf(CELLS, LO), buf(6, 49, 8, LO),
        buf(256, HID, dtype=BF16), buf(256, HID, dtype=BF16),
        buf(256, HID), buf(CH, HID), buf(2, 49, 8, LO), buf(2 * HALF, LO),
        buf(HALF, LO, dtype=BF16), buf(HALF, LO, dtype=BF16),
        buf(16, PIECE, LO, dtype=BF16), buf(15, PIECE, LO, dtype=BF16), buf(4, PIECE, LO),
        buf(2, 16, PIECE, LO, dtype=BF16),
        pltpu.SemaphoreType.DMA((COPIES,)), pltpu.SemaphoreType.DMA((COPIES,)),
    ]
    outs = (
        jax.ShapeDtypeStruct((ROWS, COLS, CH), BF16),
        jax.ShapeDtypeStruct((ROWS, COLS, CH), F32),
        jax.ShapeDtypeStruct((7, 7, CH), F32),
        jax.ShapeDtypeStruct((CH, HID), F32),
        jax.ShapeDtypeStruct((CH, HID), F32),
    )
    found = pl.pallas_call(
        kernel,
        out_shape=outs[:3] + (jax.ShapeDtypeStruct((2, 16, PIECE, LO), BF16),),
        in_specs=[anywhere] * 13,
        out_specs=(anywhere, anywhere, vmem, anywhere),
        scratch_shapes=scratch,
        compiler_params=pltpu.CompilerParams(
            collective_id=0, has_side_effects=True, vmem_limit_bytes=60 * 1024 * 1024
        ),
        name="block",
    )(
        states, grad_out, land_mask, partner, dw_kernel, row(dw_bias), row(ln_gain), row(ln_bias),
        w_in, b_in.reshape(HID // LO, LO), w_out.T, row(b_out), row(layer_scale),
    )
    out_a, grad_states, grad_kernel, grad_win, grad_wout = pl.pallas_call(
        finish,
        out_shape=outs,
        in_specs=[anywhere] * 4,
        out_specs=(anywhere,) * 5,
        scratch_shapes=[pltpu.VMEM(o.shape, o.dtype) for o in outs[:3]]
        + [buf(2, 16, PIECE, LO, dtype=BF16), buf(CH, HID), buf(CH, HID)]
        + [pltpu.SemaphoreType.DMA((4,)), pltpu.SemaphoreType.DMA((5,))],
        compiler_params=pltpu.CompilerParams(vmem_limit_bytes=60 * 1024 * 1024),
        name="finish",
    )(*found)
    return out_a, grad_states, grad_kernel, grad_win, grad_wout.T


def solution(mesh):
    placed = (
        P(None, "lat", "lon", None), P("lat", "lon", None), P("lat", "lon"),
        P(), P(), P(), P(), P(), P(), P(), P(), P(), P(),
    )
    return jax.shard_map(
        shards,
        mesh=mesh,
        in_specs=placed,
        out_specs=(P("lat", "lon", None), P("lat", "lon", None), P(), P(), P()),
        check_vma=False,
    )
```

```python
import functools
import math

import jax
import jax.numpy as jnp
from jax import lax
from jax.experimental import pallas as pl
from jax.experimental.pallas import tpu as pltpu
from jax.sharding import PartitionSpec as P

F32 = jnp.float32
BF16 = jnp.bfloat16
MESH = pl.DeviceIdType.MESH

ROWS = 16
COLS = 64
PROWS = 22
WIDE = 80
LO = 128
CH = 192
HID = 768
NLON = 2048
CELLS = ROWS * COLS
CHUNK = 256
PIECE = 80
HALF = 16 * PIECE
QUART = 4 * PIECE
WIN_AT, WOUT_AT, REST_AT = 0, 1152, 2304

root_factor = math.sqrt(2.0 / math.pi)
cubic_coef = 0.044715
norm_eps = 1e-06
scale = 1.0 / math.sqrt(64 * NLON)

LAT_AT, LON_AT, FIELD = 0, 2, 8
FOLD_B, FOLD_A, FOLD_Z, ROUND = 16, 30, 44, 6
S0_AT, S1_AT, S3_AT, G1_AT, G3_AT = 58, 59, 74, 77, 92
K0_AT, K1_AT, K3_AT, K4_AT = 96, 97, 112, 115
COPIES = 130


def dot(a, b, dims=((1,), (0,))):
    return lax.dot_general(a, b, (dims, ((), ())), preferred_element_type=F32)


def kernel(
    x_in, go_in, mask_in, partner_in, dw_in, dwb_in, g_in, lb_in, win_in, bin_in,
    wout_in, bout_in, ls_in,
    outa_out, gs_out, gk_ref, ag_out,
    x_ref, go_ref, mask_ref, partner_ref, dw_ref, dwb_ref, g_ref, lb_ref, win_ref, bin_ref,
    wout_ref, bout_ref, ls_ref, load_sem, wbt, wot, outa_ref, gs_ref, store_sem, gkf, kr0, ksum, kr1, kr3, kag,
    pd, pz, xb, zb, sx, sz, rlx, rlz, rcx, rcz, fb1, fa1, fz1, vb, va, vz, fb2, fya, fyz, fxa, fxz,
    dp, mb, kt, wa, wb, gw, gwo, gka, flat, b0, r0, hb, r1, r3, ag, ssem, rsem,
):
    lon = lax.axis_index("lon")
    lat = lax.axis_index("lat")
    top = lat == 3
    xx, yh, zz = lon // 8, (lon // 4) % 2, lon % 4
    yl, core = lat // 2, lat % 2
    yy = yh * 2 + yl

    def lon_of(step):
        return (lon + step + 64) % 32

    mate = (lon, lat + 1 - 2 * core)

    def plane_peer(m):
        return (((xx + m // 4) % 4) * 8 + yh * 4 + (zz + m % 4) % 4, lat)

    def third_peer(k):
        far = (yy + k) % 4
        return (xx * 8 + (far // 2) * 4 + zz, (far % 2) * 2 + core)

    place = xx * 4 + zz

    def place_of(m):
        return ((xx + m // 4) % 4) * 4 + (zz + m % 4) % 4

    block8 = lon // 4
    mirror = lon + 3 - 2 * zz
    own1 = 2 * zz - 3
    own2 = (2 * block8 + 1) % 8

    def mirror_of(v):
        return v + 3 - 2 * (v % 4)

    def fold1_to(k):
        return mirror_of(lon_of(-k))

    def fold1_from(k):
        return (mirror + k) % 32

    def fold2_peer(k):
        return ((7 - block8 + k) % 8) * 4 + zz

    def remote(src, dst, i, peer):
        return pltpu.make_async_remote_copy(
            src_ref=src, dst_ref=dst, send_sem=ssem.at[i], recv_sem=rsem.at[i],
            device_id={"lon": peer[0], "lat": peer[1]}, device_id_type=MESH,
        )

    barrier = pltpu.get_barrier_semaphore()

    def greet(peer):
        pl.semaphore_signal(
            barrier, inc=1, device_id={"lon": peer[0], "lat": peer[1]}, device_id_type=MESH
        )

    greet(mate)
    for m in range(1, 16):
        greet(plane_peer(m))
    for k in (1, 2, 3):
        greet(third_peer(k))
    for side in (-1, 1):
        greet((lon_of(side), lat))
    for dl in (-1, 1):
        @pl.when((lat + dl >= 0) & (lat + dl <= 3))
        def _():
            for side in (-1, 0, 1):
                greet((lon_of(side), lat + dl))

    @pl.when(top)
    def _():
        for k in range(6):
            @pl.when(k != own1)
            def _(k=k):
                greet((fold1_from(k), lat))
        for k in range(8):
            @pl.when(k != own2)
            def _(k=k):
                greet((fold2_peer(k), lat))

    ins = (x_in, go_in, mask_in, partner_in, dw_in, dwb_in, g_in, lb_in, win_in, bin_in,
           wout_in, bout_in, ls_in)
    held = (x_ref, go_ref, mask_ref, partner_ref, dw_ref, dwb_ref, g_ref, lb_ref, win_ref, bin_ref,
            wout_ref, bout_ref, ls_ref)
    loads = [pltpu.make_async_copy(a, b, load_sem.at[i]) for i, (a, b) in enumerate(zip(ins, held))]
    for load in loads:
        load.start()
    loads[0].wait()

    def at(plane, row, col):
        return (plane * PROWS + row) * WIDE + col

    def spread(r, carry):
        a = x_ref[0, r].astype(F32)
        b = x_ref[1, r].astype(F32)
        mix = jnp.concatenate([a[:, LO:], b[:, LO:]], axis=1)
        for plane, v in enumerate((a[:, :LO], b[:, :LO], mix)):
            pd[pl.ds(pl.multiple_of(at(plane, 3 + r, 8), 8), COLS), :] = v
            xb[plane, r] = v.astype(BF16)
        return carry

    lax.fori_loop(0, ROWS, spread, 0)

    def pack(field, send, planes):
        for plane in range(planes):
            for k in range(3):
                send[0, plane, k] = field[pl.ds(at(plane, 3, 8 + k), ROWS, stride=WIDE), :].astype(BF16)
                send[1, plane, k] = field[pl.ds(at(plane, 3, 69 + k), ROWS, stride=WIDE), :].astype(BF16)

    pack(pd, sx, 3)

    peers = 21 + jnp.where(lat > 0, 3, 0) + jnp.where(lat < 3, 3, 0)
    peers = peers + jnp.where(top, 13 - jnp.where(zz >= 2, 1, 0), 0)
    pl.semaphore_wait(barrier, peers)

    def lat_copies(base, block, got):
        return (
            (lat < 3, remote(block.at[:, 13:16], got.at[0], base + LAT_AT, (lon, lat + 1))),
            (lat > 0, remote(block.at[:, 0:3], got.at[1], base + LAT_AT + 1, (lon, lat - 1))),
        )

    def lon_copies(base, send, got):
        found = []
        for side in range(2):
            for slot in range(3):
                dl = 1 - slot
                found.append((
                    (lat + dl >= 0) & (lat + dl <= 3),
                    remote(
                        send.at[1 - side], got.at[side, slot], base + LON_AT + 3 * side + slot,
                        (lon_of(1 - 2 * side), lat + dl),
                    ),
                ))
        return found

    def lon_arrives(slot):
        return (lat + slot - 1 >= 0) & (lat + slot - 1 <= 3)

    def fold1_copies(base, block, planes, got):
        found = []
        for k in range(6):
            width = 16 if k == 5 else COLS
            found.append((k != own1, remote(
                block.at[planes, 13:16, 0:width], got.at[k, :, :, 0:width], base + k,
                (fold1_to(k), lat),
            )))
        return found

    def fold2_copies(base, window, got):
        return [
            (k != own2, remote(window, got.at[k], base + ROUND + k, (fold2_peer(k), lat)))
            for k in range(8)
        ]

    def start_fold(base, block, planes, f1):
        for cond, copy in fold1_copies(base, block, planes, f1):
            pl.when(cond)(copy.start)

    def start_halo(base, block, send, rl, rc):
        for cond, copy in lon_copies(base, send, rc):
            pl.when(cond)(copy.start)
        for cond, copy in lat_copies(base, block, rl):
            pl.when(cond)(copy.start)

    def finish_halo(base, field, planes, block, send, rl, rc):
        lats = lat_copies(base, block, rl)
        for way, (arrives, row) in enumerate(((lat > 0, 0), (lat < 3, 19))):
            @pl.when(arrives)
            def _(way=way, row=row):
                lats[way][1].wait_recv()
                for plane in range(planes):
                    for r in range(3):
                        field[pl.ds(at(plane, row + r, 8), COLS), :] = rl[way, plane, r].astype(F32)
        lons = lon_copies(base, send, rc)
        for side in range(2):
            col = 5 if side == 0 else 72
            for slot in range(3):
                @pl.when(lon_arrives(slot))
                def _(side=side, slot=slot, col=col):
                    lons[3 * side + slot][1].wait_recv()
                    for plane in range(planes):
                        for k in range(3):
                            v = rc[side, slot, plane, k].astype(F32)
                            if slot == 1:
                                field[pl.ds(at(plane, 3, col + k), ROWS, stride=WIDE), :] = v
                            else:
                                for r in range(3):
                                    row = r if slot == 0 else 19 + r
                                    own = 13 + r if slot == 0 else r
                                    field[pl.ds(at(plane, row, col + k), 1), :] = v[own:own + 1]

    def shift_parts():
        begin = lax.rem(partner_ref[0] + (NLON - 2), NLON)
        return lax.rem(begin, COLS), lax.rem(lax.div(begin, COLS), 4), lax.div(begin, 4 * COLS)

    def make_window(base, block, planes, f1, window):
        offset, near, _ = shift_parts()
        for cond, copy in fold1_copies(base, block, planes, f1):
            pl.when(cond)(copy.wait_recv)

        @pl.when(zz >= 2)
        def _():
            f1[own1] = block[planes, 13:16]

        slot_at = lax.broadcasted_iota(jnp.int32, (WIDE, 3 * COLS), 0)
        from_at = lax.broadcasted_iota(jnp.int32, (WIDE, 3 * COLS), 1)
        pick = jnp.where(from_at + slot_at == offset + 74, 1.0, 0.0).astype(BF16)
        for plane in range(window.shape[0]):
            for r in range(3):
                three = jnp.concatenate([f1[near + c, plane, r] for c in range(3)], axis=0)
                window[plane, r] = dot(pick, three).astype(BF16)

    def middle_fold(base, block, planes, f1, window, f2):
        make_window(base, block, planes, f1, window)
        for cond, copy in fold2_copies(base, window, f2):
            pl.when(cond)(copy.start)
        f2[own2] = window[...]

    def foldy_copy(base, window, fy):
        return remote(window, fy.at[yh], base + ROUND, (xx * 8 + (1 - yh) * 4 + zz, lat))

    def foldy_from(base, window, fy):
        return remote(window, fy.at[1 - yh], base + ROUND, (xx * 8 + (1 - yh) * 4 + zz, lat))

    def foldx_copies(base, fy, fx):
        return [
            remote(fy.at[2], fx.at[xx], base + ROUND + k, (((xx + k) % 4) * 8 + yh * 4 + zz, lat))
            for k in (1, 2, 3)
        ]

    def foldx_from(base, fy, fx):
        return [
            remote(fy.at[2], fx.at[(xx + 4 - k) % 4], base + ROUND + k, (((xx + k) % 4) * 8 + yh * 4 + zz, lat))
            for k in (1, 2, 3)
        ]

    def fold_to_y(base, block, planes, f1, window, fy):
        make_window(base, block, planes, f1, window)
        foldy_copy(base, window, fy).start()
        fy[yh] = window[...]

    def fold_to_x(base, window, fy, fx):
        foldy_from(base, window, fy).wait_recv()
        far = shift_parts()[2]
        chosen = fy[lax.rem(1 - yh + far, 2)]
        fy[2] = chosen
        for copy in foldx_copies(base, fy, fx):
            copy.start()
        fx[xx] = chosen

    def end_fold(base, field, first, fy, fx):
        for copy in foldx_from(base, fy, fx):
            copy.wait_recv()
        far = shift_parts()[2]
        source = lax.div(lax.rem(7 - block8 + far, 8), 2)
        for plane in range(fx.shape[1]):
            for k in range(3):
                field[pl.ds(at(first + plane, 19 + k, 0), WIDE), :] = fx[source, plane, 2 - k].astype(F32)

    def close_three(base, block, planes, f1, window, fy, fx):
        for cond, copy in fold1_copies(base, block, planes, f1):
            pl.when(cond)(copy.wait_send)
        foldy_copy(base, window, fy).wait_send()
        for copy in foldx_copies(base, fy, fx):
            copy.wait_send()

    def finish_fold(base, field, first, window, f2):
        for cond, copy in fold2_copies(base, window, f2):
            pl.when(cond)(copy.wait_recv)
        far = shift_parts()[2]
        for plane in range(window.shape[0]):
            for k in range(3):
                field[pl.ds(at(first + plane, 19 + k, 0), WIDE), :] = f2[far, plane, 2 - k].astype(F32)

    def close_fold(base, block, planes, f1, window, f2):
        for cond, copy in fold1_copies(base, block, planes, f1):
            pl.when(cond)(copy.wait_send)
        for cond, copy in fold2_copies(base, window, f2):
            pl.when(cond)(copy.wait_send)

    def close_field(base, block, send, rl, rc):
        for cond, copy in lat_copies(base, block, rl):
            pl.when(cond)(copy.wait_send)
        for cond, copy in lon_copies(base, send, rc):
            pl.when(cond)(copy.wait_send)

    in_b, in_a, in_z = slice(1, 3), slice(0, 1), slice(0, 2)

    @pl.when(top)
    def _():
        start_fold(FOLD_B, xb, in_b, fb1)

    start_halo(0, xb, sx, rlx, rcx)

    for load in loads[1:]:
        load.wait()

    def clear_south(field, planes):
        for plane in range(planes):
            field[pl.ds(at(plane, 0, 0), 3 * WIDE), :] = jnp.zeros((3 * WIDE, LO), F32)

    clear_south(pd, 3)
    clear_south(pz, 2)

    lane = lax.broadcasted_iota(jnp.int32, (1, LO), 1)
    upper = lane >= 64

    def table(a, carry):
        low, high = dw_ref[a][:, :LO], dw_ref[a][:, LO:]
        mix = jnp.concatenate([high, high], axis=1)
        rlow, rhigh = dw_ref[6 - a][:, :LO], dw_ref[6 - a][:, LO:]
        rmix = jnp.concatenate([rhigh, rhigh], axis=1)
        for b in range(7):
            for kind, (v, w) in enumerate(((low, rlow), (mix, rmix))):
                straight = jnp.broadcast_to(v[b:b + 1], (8, LO))
                turned = jnp.broadcast_to(w[6 - b:7 - b], (8, LO))
                kt[kind, a * 7 + b] = straight
                kt[2 + kind, a * 7 + b] = turned
                kt[4 + kind, a * 7 + b] = jnp.where(top, straight, turned)
        return carry

    lax.fori_loop(0, 7, table, 0)
    wa[0:192] = win_ref[...]
    wa[192:256] = jnp.zeros((64, HID), BF16)
    wb[0:128] = win_ref[0:128]
    wb[128:192] = jnp.zeros((64, HID), BF16)
    wb[192:256] = win_ref[128:192]
    for n in range(3):
        part = slice(256 * n, 256 * n + 256)
        wbt[part] = wb[:, part].T
        both = jnp.concatenate([wout_ref[:, part], jnp.zeros((64, 256), BF16)], axis=0)
        wot[part] = both.T[:, 0:CH]
    eye = jnp.where(
        lax.broadcasted_iota(jnp.int32, (COLS, COLS), 0) == lax.broadcasted_iota(jnp.int32, (COLS, COLS), 1),
        1.0, 0.0,
    ).astype(BF16)
    mask_t = dot(eye, mask_ref[...].astype(F32).astype(BF16), ((1,), (1,))).astype(BF16)
    for r in range(ROWS):
        one = jnp.where(lax.broadcasted_iota(jnp.int32, (ROWS, LO), 0) == r, 1.0, 0.0).astype(BF16)
        mb[r * COLS:(r + 1) * COLS] = dot(mask_t, one)
    gw[...] = jnp.zeros_like(gw)
    gwo[...] = jnp.zeros_like(gwo)
    gka[...] = jnp.zeros_like(gka)
    flat[REST_AT:2560] = jnp.zeros((2560 - REST_AT, LO), F32)
    gkf[112:128] = jnp.zeros((16, LO), F32)
    for f1 in (fb1, fa1, fz1):
        f1[5, :, :, 16:64] = jnp.zeros_like(f1[5, :, :, 16:64])


    zero64 = jnp.zeros((1, 64), F32)

    def halves(ref, state):
        v = ref[...]
        high = v[:, LO:]
        parts = [high, zero64] if state == 0 else [zero64, high]
        return v[:, :LO], jnp.concatenate(parts, axis=1)

    def conv(field, plane, c, half, tab, tab_last):
        base = at(plane, 4 * c, 32 * half + 5)
        acc = [[jnp.zeros((8, LO), F32) for _ in range(4)] for _ in range(4)]
        for p in range(10):
            for b in range(7):
                use = tab_last if p >= 7 else tab
                ks = {r: kt[use, (p - r) * 7 + b] for r in range(4) if 0 <= p - r <= 6}
                for t in range(4):
                    v = field[pl.ds(base + p * WIDE + 8 * t + b, 8), :]
                    for r, kv in ks.items():
                        acc[r][t] = acc[r][t] + kv * v
        return acc

    def bias(s):
        return jnp.concatenate([bin_ref[2 * s:2 * s + 1], bin_ref[2 * s + 1:2 * s + 2]], axis=1)

    def norm(c, state):
        here = pl.ds(pl.multiple_of(c * CHUNK, CHUNK), CHUNK)
        keep = upper if state == 1 else jnp.logical_not(upper)
        blo, bhi = halves(dwb_ref, state)
        glo, ghi = halves(g_ref, state)
        llo, lhi = halves(lb_ref, state)
        lo = dp[state, here] + blo
        hi = jnp.where(keep, dp[2, here] + bhi, 0.0)
        mean = jnp.sum(lo + hi, axis=1, keepdims=True) * (1.0 / CH)
        lo = lo - mean
        hi = jnp.where(keep, hi - mean, 0.0)
        inv = lax.rsqrt(jnp.sum(lo * lo + hi * hi, axis=1, keepdims=True) * (1.0 / CH) + norm_eps)
        nlo, nhi = lo * inv, hi * inv
        low = jnp.concatenate(
            [(nlo * glo + llo).astype(BF16), (nhi * ghi + lhi).astype(BF16)], axis=1
        )
        return low, nlo, nhi, inv, glo, ghi, keep

    def forward_chunk(c):
        low = norm(c, 0)[0]
        mixed = jnp.broadcast_to(bout_ref[...], (CHUNK, CH))
        for s in range(3):
            cut = slice(256 * s, 256 * s + 256)
            u = dot(low, wa[:, cut]) + bias(s)
            t = jnp.tanh(u * (root_factor + (root_factor * cubic_coef) * (u * u)))
            act = (u * (0.5 + 0.5 * t)).astype(BF16)
            mixed = mixed + dot(act, wot[cut])
        mixed = mixed * ls_ref[...]
        here = pl.ds(pl.multiple_of(c * CHUNK, CHUNK), CHUNK)
        m = mb[here]
        mm = jnp.concatenate([m, m[:, :64]], axis=1)
        for r in range(4):
            cut = slice(64 * r, 64 * r + 64)
            outa_ref[4 * c + r] = (x_ref[0, 4 * c + r].astype(F32) + mm[cut] * mixed[cut]).astype(BF16)

    def backward_chunk(c):
        low, nlo, nhi, inv, glo, ghi, keep = norm(c, 1)
        here = pl.ds(pl.multiple_of(c * CHUNK, CHUNK), CHUNK)
        m = mb[here]
        mm = jnp.concatenate([m, m[:, :64]], axis=1)
        go = jnp.concatenate([go_ref[4 * c + r] for r in range(4)], axis=0).astype(F32)
        gl = (mm * (ls_ref[...] * go)).astype(BF16)
        low_t = low.T
        gl_t = jnp.concatenate([gl, jnp.zeros((CHUNK, 64), BF16)], axis=1).T[0:CH]
        gn = jnp.zeros((CHUNK, 256), F32)
        for s in range(3):
            cut = slice(256 * s, 256 * s + 256)
            u = dot(low, wb[:, cut]) + bias(s)
            u2 = u * u
            t = jnp.tanh(u * (root_factor + (root_factor * cubic_coef) * u2))
            half = 0.5 + 0.5 * t
            value = u * half
            slope = half + value * (1.0 - t) * (root_factor + (3.0 * root_factor * cubic_coef) * u2)
            act = value.astype(BF16)
            gwo[:, cut] += dot(gl_t, act)
            gh = (dot(gl, wout_ref[:, cut]) * slope).astype(BF16)
            gw[:, cut] += dot(low_t, gh)
            gn = gn + dot(gh, wbt[cut])
        nl, nh = gn[:, :LO] * glo, gn[:, LO:] * ghi
        one = jnp.sum(nl + nh, axis=1, keepdims=True) * (1.0 / CH)
        two = jnp.sum(nl * nlo + nh * nhi, axis=1, keepdims=True) * (1.0 / CH)
        zl = inv * (nl - one - nlo * two)
        zh = jnp.where(keep, inv * (nh - one - nhi * two), 0.0)
        for plane, v in enumerate((zl, zh)):
            for r in range(4):
                cut = slice(64 * r, 64 * r + 64)
                pz[pl.ds(pl.multiple_of(at(plane, 3 + 4 * c + r, 8), 8), COLS), :] = v[cut]
                zb[plane, 4 * c + r] = v[cut].astype(BF16)

    def sweep_states(plane, c):
        def sweep(half, carry):
            kind = plane // 2
            acc = conv(pd, plane, c, half, kind, kind)
            for r in range(4):
                for t in range(4):
                    cell = pl.multiple_of(c * CHUNK + r * COLS + half * 32 + 8 * t, 8)
                    dp[plane, pl.ds(cell, 8)] = acc[r][t]
            return carry

        lax.fori_loop(0, 2, sweep, 0)

    def kernel_chunk(c):
        for plane in range(2):
            for rows in ((0, 1, 2, 3), (4, 5, 6)):
                def add_row(i, acc, plane=plane, rows=rows):
                    acc = list(acc)
                    for t in range(8):
                        z = pz[pl.ds(pl.multiple_of(at(plane, 3 + i, 8 + 8 * t), 8), 8), :]
                        for n, a in enumerate(rows):
                            for b in range(7):
                                v = pd[pl.ds(at(1 + plane, i + a, 5 + 8 * t + b), 8), :]
                                acc[n * 7 + b] = acc[n * 7 + b] + v * z
                    return tuple(acc)

                acc = lax.fori_loop(
                    4 * c, 4 * c + 4, add_row,
                    tuple(jnp.zeros((8, LO), F32) for _ in range(7 * len(rows))),
                )
                for n, a in enumerate(rows):
                    for b in range(7):
                        gka[plane, a * 7 + b] += acc[n * 7 + b]

    @pl.when(top)
    def _():
        middle_fold(FOLD_B, xb, in_b, fb1, vb, fb2)

    finish_halo(0, pd, 3, xb, sx, rlx, rcx)

    def first_pass(c, carry):
        @pl.when(top & (c == 2))
        def _():
            start_fold(FOLD_A, xb, in_a, fa1)

        @pl.when(top & (c == 3))
        def _():
            finish_fold(FOLD_B, pd, 1, vb, fb2)

        def both(plane, carry):
            sweep_states(plane, c)
            return carry

        lax.fori_loop(1, 3, both, 0)

        backward_chunk(c)
        return carry

    lax.fori_loop(0, 4, first_pass, 0)

    for s in range(6):
        cut = slice(128 * s, 128 * s + 128)
        flat[WIN_AT + 192 * s:WIN_AT + 192 * s + 128] = gw[0:128, cut]
        flat[WIN_AT + 192 * s + 128:WIN_AT + 192 * s + 192] = gw[192:256, cut]
        flat[WOUT_AT + 192 * s:WOUT_AT + 192 * s + 192] = gwo[:, cut]

    def half_at(which):
        return pl.ds(pl.multiple_of(which * HALF, 8), HALF)

    b0[...] = flat[half_at(1 - core)].astype(BF16)
    s0 = remote(b0, r0, S0_AT, mate)

    def s1(m):
        return remote(hb.at[place_of(m)], r1.at[m - 1], S1_AT + m - 1, plane_peer(m))

    def s3(k):
        return remote(r3.at[yy], r3.at[yy], S3_AT + k - 1, third_peer(k))

    def s3_from(k):
        return remote(r3.at[yy], r3.at[(yy + 4 - k) % 4], S3_AT + k - 1, third_peer(k))

    def g1(m):
        return remote(ag.at[core, place], ag.at[core, place], G1_AT + m - 1, plane_peer(m))

    def g1_from(m):
        there = ((xx + 4 - m // 4) % 4) * 4 + (zz + 4 - m % 4) % 4
        return remote(ag.at[core, place], ag.at[core, there], G1_AT + m - 1, plane_peer(m))

    def g3(d):
        rows = pl.ds(pl.multiple_of(((xx + 4 - d) % 4) * 4, 4), 4)
        return remote(ag.at[core, rows], ag.at[core, rows], G3_AT + d, mate)

    def g3_from(d):
        rows = pl.ds(pl.multiple_of(((xx + 4 - d) % 4) * 4, 4), 4)
        return remote(ag.at[core, rows], ag.at[1 - core, rows], G3_AT + d, mate)

    k0 = remote(gkf, kr0, K0_AT, mate)

    def k1(m):
        return remote(ksum.at[place_of(m)], kr1.at[m - 1], K1_AT + m - 1, plane_peer(m))

    def k3(k):
        return remote(kr3.at[yy], kr3.at[yy], K3_AT + k - 1, third_peer(k))

    def k3_from(k):
        return remote(kr3.at[yy], kr3.at[(yy + 4 - k) % 4], K3_AT + k - 1, third_peer(k))

    def k4(m):
        return remote(kag.at[place], kag.at[place], K4_AT + m - 1, plane_peer(m))

    def k4_from(m):
        there = ((xx + 4 - m // 4) % 4) * 4 + (zz + 4 - m % 4) % 4
        return remote(kag.at[place], kag.at[there], K4_AT + m - 1, plane_peer(m))

    s0.start()

    pack(pz, sz, 2)

    @pl.when(top)
    def _():
        start_fold(FOLD_Z, zb, in_z, fz1)

    start_halo(FIELD, zb, sz, rlz, rcz)

    def second_pass(c, carry):
        @pl.when(c == 2)
        def _():
            s0.wait_recv()
            for i in range(16):
                part = pl.ds(pl.multiple_of(core * HALF + i * PIECE, 8), PIECE)
                total = flat[part] + r0[i * PIECE:(i + 1) * PIECE].astype(F32)
                flat[part] = total
                hb[i] = total.astype(BF16)
            for m in range(1, 16):
                s1(m).start()

        @pl.when(top & (c == 2))
        def _():
            fold_to_y(FOLD_A, xb, in_a, fa1, va, fya)

        kernel_chunk(c)
        return carry

    lax.fori_loop(0, 4, second_pass, 0)

    for plane in range(2):
        for n in range(49):
            line = plane * 56 + n
            gkf[line:line + 1] = jnp.sum(gka[plane, n], axis=0, keepdims=True)
        gkf[plane * 56 + 49:plane * 56 + 56] = jnp.zeros((7, LO), F32)
    k0.start()

    def state_pass(c, carry):
        @pl.when(c == 2)
        def _():
            k0.wait_recv()
            for i in range(16):
                ksum[i] = gkf[8 * i:8 * i + 8] + kr0[8 * i:8 * i + 8]
            for m in range(1, 16):
                k1(m).start()

        sweep_states(0, c)
        forward_chunk(c)
        return carry

    lax.fori_loop(0, 3, state_pass, 0)

    finish_halo(FIELD, pz, 2, zb, sz, rlz, rcz)

    @pl.when(top)
    def _():
        fold_to_y(FOLD_Z, zb, in_z, fz1, vz, fyz)

    stores = [
        pltpu.make_async_copy(outa_ref, outa_out, store_sem.at[0]),
        pltpu.make_async_copy(gs_ref, gs_out, store_sem.at[1]),
        pltpu.make_async_copy(ag.at[core], ag_out.at[core], store_sem.at[2]),
        pltpu.make_async_copy(ag.at[1 - core], ag_out.at[1 - core], store_sem.at[3]),
    ]

    def third_pass(c, carry):
        @pl.when(top & (c == 1))
        def _():
            fold_to_x(FOLD_A, va, fya, fxa)

        @pl.when(c == 1)
        def _():
            for m in range(1, 16):
                s1(m).wait_recv()
            total = flat[pl.ds(pl.multiple_of(core * HALF + place * PIECE, 8), PIECE)]
            for m in range(15):
                total = total + r1[m].astype(F32)
            r3[yy] = total
            for k in (1, 2, 3):
                s3(k).start()

        @pl.when(c == 2)
        def _():
            for m in range(1, 16):
                k1(m).wait_recv()
            total = ksum[place]
            for m in range(15):
                total = total + kr1[m]
            kr3[yy] = total
            for k in (1, 2, 3):
                k3(k).start()

        @pl.when(top & (c == 2))
        def _():
            fold_to_x(FOLD_Z, vz, fyz, fxz)

        @pl.when(c == 3)
        def _():
            for k in (1, 2, 3):
                s3_from(k).wait_recv()
            ag[core, place] = ((r3[0] + r3[1] + r3[2] + r3[3]) * scale).astype(BF16)
            for m in range(1, 16):
                g1(m).start()

        @pl.when(top & (c == 3))
        def _():
            end_fold(FOLD_A, pd, 0, fya, fxa)

        @pl.when(c == 3)
        def _():
            sweep_states(0, 3)
            forward_chunk(3)
            stores[0].start()
            for k in (1, 2, 3):
                k3_from(k).wait_recv()
            kag[place] = (kr3[0] + kr3[1] + kr3[2] + kr3[3]) * scale
            for m in range(1, 16):
                k4(m).start()

        @pl.when(top & (c == 3))
        def _():
            end_fold(FOLD_Z, pz, 0, fyz, fxz)

        last = jnp.where(c == 3, 4, 2)

        def sweep(half, carry):
            at_col = pl.ds(pl.multiple_of(32 * half, 32), 32)
            acc_lo = conv(pz, 0, c, half, 2, last)
            for r in range(4):
                low = jnp.concatenate(acc_lo[r], axis=0)
                go = go_ref[4 * c + r, at_col, :].astype(F32)
                gs_ref[4 * c + r, at_col, 0:LO] = low + go[:, :LO]
            acc_hi = conv(pz, 1, c, half, 3, last + 1)
            for r in range(4):
                high = jnp.concatenate(acc_hi[r], axis=0)
                go = go_ref[4 * c + r, at_col, :].astype(F32)
                gs_ref[4 * c + r, at_col, LO:CH] = high[:, 64:] + go[:, LO:]
            return carry

        lax.fori_loop(0, 2, sweep, 0)
        return carry

    lax.fori_loop(0, 4, third_pass, 0)

    stores[1].start()
    for d in (0, 1, 3, 2):
        for m in range(max(4 * d, 1), 4 * d + 4):
            g1_from(m).wait_recv()
        g3(d).start()
    stores[2].start()
    for m in range(1, 16):
        k4_from(m).wait_recv()
    kall = jnp.concatenate([kag[i] for i in range(14)], axis=0)
    for a in range(7):
        gk_ref[a, :, 0:LO] = kall[7 * a:7 * a + 7]
        gk_ref[a, :, LO:CH] = kall[56 + 7 * a:56 + 7 * a + 7, 64:]
    for d in range(4):
        g3_from(d).wait_recv()
    stores[3].start()

    close_field(0, xb, sx, rlx, rcx)
    close_field(FIELD, zb, sz, rlz, rcz)

    @pl.when(top)
    def _():
        close_fold(FOLD_B, xb, in_b, fb1, vb, fb2)
        close_three(FOLD_A, xb, in_a, fa1, va, fya, fxa)
        close_three(FOLD_Z, zb, in_z, fz1, vz, fyz, fxz)

    s0.wait_send()
    for m in range(1, 16):
        s1(m).wait_send()
        g1(m).wait_send()
    for k in (1, 2, 3):
        s3(k).wait_send()
    for d in range(4):
        g3(d).wait_send()
    k0.wait_send()
    for m in range(1, 16):
        k1(m).wait_send()
        k4(m).wait_send()
    for k in (1, 2, 3):
        k3(k).wait_send()
    for store in stores:
        store.wait()


def part_of(ag, start, size):
    first, end = start // PIECE, -(-(start + size) // PIECE)
    found = [ag[i // 16, i % 16] for i in range(first, end)]
    return jnp.concatenate(found, axis=0)[start - first * PIECE:start - first * PIECE + size].astype(F32)


def finish(
    outa_in, gs_in, gk_in, ag_in, outa_out, gs_out, gk_out, gwin_out, gwout_out,
    outa, gs, gk, ag, gwin, gwout, come, go,
):
    first = [
        pltpu.make_async_copy(a, b, come.at[i])
        for i, (a, b) in enumerate(((ag_in, ag), (gs_in, gs), (outa_in, outa), (gk_in, gk)))
    ]
    second = [
        pltpu.make_async_copy(a, b, go.at[i])
        for i, (a, b) in enumerate(((gs, gs_out), (outa, outa_out), (gk, gk_out), (gwin, gwin_out), (gwout, gwout_out)))
    ]
    for copy in first:
        copy.start()
    first[0].wait()
    for s in range(6):
        gwin[:, 128 * s:128 * s + 128] = part_of(ag, WIN_AT + 192 * s, 192)
    second[3].start()
    for i in range(3):
        first[i + 1].wait()
        second[i].start()
    for s in range(6):
        gwout[:, 128 * s:128 * s + 128] = part_of(ag, WOUT_AT + 192 * s, 192)
    second[4].start()
    for copy in second:
        copy.wait()


def shards(states, grad_out, land_mask, partner, dw_kernel, dw_bias, ln_gain, ln_bias, w_in, b_in,
           w_out, b_out, layer_scale):
    def row(v):
        return v.reshape(1, v.shape[0])

    vmem = pl.BlockSpec(memory_space=pltpu.VMEM)
    anywhere = pl.BlockSpec(memory_space=pl.ANY)

    def buf(*shape, dtype=F32):
        return pltpu.VMEM(shape, dtype)

    load_to = [
        buf(2, ROWS, COLS, CH, dtype=BF16), buf(ROWS, COLS, CH, dtype=BF16),
        buf(ROWS, COLS, dtype=jnp.int32), pltpu.SMEM((NLON,), jnp.int32), buf(7, 7, CH),
        buf(1, CH), buf(1, CH), buf(1, CH), buf(CH, HID, dtype=BF16), buf(HID // LO, LO),
        buf(CH, HID, dtype=BF16), buf(1, CH), buf(1, CH), pltpu.SemaphoreType.DMA((13,)),
        buf(HID, 256, dtype=BF16), buf(HID, CH, dtype=BF16),
        buf(ROWS, COLS, CH, dtype=BF16), buf(ROWS, COLS, CH), pltpu.SemaphoreType.DMA((4,)),
        buf(128, LO), buf(128, LO), buf(16, 8, LO), buf(15, 8, LO), buf(4, 8, LO), buf(16, 8, LO),
    ]
    scratch = load_to + [
        buf(3 * PROWS * WIDE, LO), buf(2 * PROWS * WIDE, LO),
        buf(3, ROWS, COLS, LO, dtype=BF16), buf(2, ROWS, COLS, LO, dtype=BF16),
        buf(2, 3, 3, ROWS, LO, dtype=BF16), buf(2, 2, 3, ROWS, LO, dtype=BF16),
        buf(2, 3, 3, COLS, LO, dtype=BF16), buf(2, 2, 3, COLS, LO, dtype=BF16),
        buf(2, 3, 3, 3, ROWS, LO, dtype=BF16), buf(2, 3, 2, 3, ROWS, LO, dtype=BF16),
        buf(6, 2, 3, COLS, LO, dtype=BF16), buf(6, 1, 3, COLS, LO, dtype=BF16),
        buf(6, 2, 3, COLS, LO, dtype=BF16),
        buf(2, 3, WIDE, LO, dtype=BF16), buf(1, 3, WIDE, LO, dtype=BF16), buf(2, 3, WIDE, LO, dtype=BF16),
        buf(8, 2, 3, WIDE, LO, dtype=BF16),
        buf(3, 1, 3, WIDE, LO, dtype=BF16), buf(3, 2, 3, WIDE, LO, dtype=BF16),
        buf(4, 1, 3, WIDE, LO, dtype=BF16), buf(4, 2, 3, WIDE, LO, dtype=BF16),
        buf(3, CELLS, LO), buf(CELLS, LO), buf(6, 49, 8, LO),
        buf(256, HID, dtype=BF16), buf(256, HID, dtype=BF16),
        buf(256, HID), buf(CH, HID), buf(2, 49, 8, LO), buf(2 * HALF, LO),
        buf(HALF, LO, dtype=BF16), buf(HALF, LO, dtype=BF16),
        buf(16, PIECE, LO, dtype=BF16), buf(15, PIECE, LO, dtype=BF16), buf(4, PIECE, LO),
        buf(2, 16, PIECE, LO, dtype=BF16),
        pltpu.SemaphoreType.DMA((COPIES,)), pltpu.SemaphoreType.DMA((COPIES,)),
    ]
    outs = (
        jax.ShapeDtypeStruct((ROWS, COLS, CH), BF16),
        jax.ShapeDtypeStruct((ROWS, COLS, CH), F32),
        jax.ShapeDtypeStruct((7, 7, CH), F32),
        jax.ShapeDtypeStruct((CH, HID), F32),
        jax.ShapeDtypeStruct((CH, HID), F32),
    )
    found = pl.pallas_call(
        kernel,
        out_shape=outs[:3] + (jax.ShapeDtypeStruct((2, 16, PIECE, LO), BF16),),
        in_specs=[anywhere] * 13,
        out_specs=(anywhere, anywhere, vmem, anywhere),
        scratch_shapes=scratch,
        compiler_params=pltpu.CompilerParams(
            collective_id=0, has_side_effects=True, vmem_limit_bytes=60 * 1024 * 1024
        ),
        name="block",
    )(
        states, grad_out, land_mask, partner, dw_kernel, row(dw_bias), row(ln_gain), row(ln_bias),
        w_in, b_in.reshape(HID // LO, LO), w_out.T, row(b_out), row(layer_scale),
    )
    out_a, grad_states, grad_kernel, grad_win, grad_wout = pl.pallas_call(
        finish,
        out_shape=outs,
        in_specs=[anywhere] * 4,
        out_specs=(anywhere,) * 5,
        scratch_shapes=[pltpu.VMEM(o.shape, o.dtype) for o in outs[:3]]
        + [buf(2, 16, PIECE, LO, dtype=BF16), buf(CH, HID), buf(CH, HID)]
        + [pltpu.SemaphoreType.DMA((4,)), pltpu.SemaphoreType.DMA((5,))],
        compiler_params=pltpu.CompilerParams(vmem_limit_bytes=60 * 1024 * 1024),
        name="finish",
    )(*found)
    return out_a, grad_states, grad_kernel, grad_win, grad_wout.T


def solution(mesh):
    placed = (
        P(None, "lat", "lon", None), P("lat", "lon", None), P("lat", "lon"),
        P(), P(), P(), P(), P(), P(), P(), P(), P(), P(),
    )
    return jax.shard_map(
        shards,
        mesh=mesh,
        in_specs=placed,
        out_specs=(P("lat", "lon", None), P("lat", "lon", None), P(), P(), P()),
        check_vma=False,
    )
```
